256 devices in a mesh: occi: 8 (over z_lo, y), occj: 32 (over x, z_hi, core).
Axes of the slice: x: 4, y: 4, z: 8 (z_hi: 4, z_lo: 2; z = z_hi * 2 + z_lo), core: 2. Of those that a mesh axis runs over, the one named last changes fastest.
Arguments:
- amplitudes: float32 [256, 768, 768], P(('occi', 'occj')), may hold values from -6 to 6
- first_rotation: float32 [768, 768], replicated, may hold values from -0.21875 to 0.21875
- second_rotation: float32 [768, 768], replicated, may hold values from -0.21875 to 0.21875
- pair_weights: float32 [16, 16], replicated, may hold values from -1.5 to 1.5
- denominators: float32 [16, 16, 768, 768], P('occi', None, 'occj'), may hold values from 1 to 4
Outputs:
- update: float32 [16, 16, 768, 768], P('occi', None, 'occj')
The draws below stay inside these ranges and needn't reach their ends.
All inputs are finite; a program needn't handle non-finite values.
Results may differ from the reference program's by a relative error of at most 0.00007.
Values sent between devices are 32-bit elements; how exact they have to be, the bound alone decides.
No kernel may reach another device: no remote copies, remote signals or barrier semaphores. Data moves between devices by JAX's collectives and lax.ppermute only.
A program may use at most 64 MiB of HBM per device.

```python
import jax
import jax.numpy as jnp
from jax import lax

OCC = 16
VIRT = 768


def block_levels(key, shape, pieces, smallest, top_value):
    def one(dim, parts):
        heights = jax.random.uniform(jax.random.fold_in(jax.random.fold_in(key, 6), dim), (parts,), jnp.float32, smallest / len(pieces), top_value / len(pieces))
        return jnp.repeat(jnp.exp(heights), shape[dim] // parts).reshape((-1,) + (1,) * (len(shape) - dim - 1))

    loudness = one(*pieces[0])
    for cut in pieces[1:]:
        loudness = loudness * one(*cut)
    return loudness


def normal_values(stream_key, dims, scale, reach, pieces=(), held_as=jnp.bfloat16):
    gain = block_levels(stream_key, dims, pieces, -0.22, 0.18) if pieces else 1.0
    array = jax.random.normal(stream_key, dims, jnp.float32) * scale * gain
    return jnp.minimum(jnp.maximum(array, -reach), reach).astype(held_as)


def setup_inputs(seed: int = 0) -> dict:
    key_list = jax.random.split(jax.random.key(seed), 6)
    return {
        "amplitudes": normal_values(key_list[0], (OCC * OCC, VIRT, VIRT), 1.0, 6.0, ((0, 256),), jnp.float32),
        "first_rotation": normal_values(key_list[1], (VIRT, VIRT), VIRT ** -0.5, 0.21875, (), jnp.float32),
        "second_rotation": normal_values(key_list[2], (VIRT, VIRT), VIRT ** -0.5, 0.21875, (), jnp.float32),
        "pair_weights": normal_values(key_list[3], (OCC, OCC), OCC ** -0.5, 1.5, (), jnp.float32),
        "denominators": jnp.clip(1.0 + 3.0 * jax.random.uniform(key_list[4], (OCC, OCC, VIRT, VIRT), jnp.float32) ** block_levels(key_list[4], (OCC, OCC, VIRT, VIRT), ((0, 8), (2, 32)), -0.2, 0.2), 1.0, 4.0),
    }


def reference(amplitudes, first_rotation, second_rotation, pair_weights, denominators):
    highest = lax.Precision.HIGHEST
    blocks = amplitudes.reshape(OCC, OCC, VIRT, VIRT)

    def transform(pair_group):
        halfway = jnp.einsum("ac,jcd->jad", first_rotation, pair_group, precision=highest)
        return jnp.einsum("jad,bd->jab", halfway, second_rotation, precision=highest)

    finished = lax.map(transform, blocks)
    summed = jnp.transpose(finished, (0, 1, 3, 2)) + jnp.transpose(finished, (1, 0, 2, 3))
    contracted = jnp.einsum("jk,ijba->ikba", pair_weights, summed, precision=highest)
    return contracted / denominators
```

```python
import jax
import jax.numpy as jnp
from jax import lax
from jax.experimental import pallas as pl
from jax.experimental.pallas import tpu as pltpu
from jax.sharding import PartitionSpec as P

OCC = 16
VIRT = 768
ROWS = 8
COLS = 32
WIDTH = VIRT // COLS
HALF = VIRT // 2
CHUNK = 256
F32 = jnp.float32
BF16 = jnp.bfloat16
NT = (((1,), (1,)), ((), ()))
NN = (((1,), (0,)), ((), ()))


def halves(x):
    high = x.astype(BF16)
    return high, (x - high.astype(F32)).astype(BF16)


def dot3(lh, ll, rh, rl, dims):
    def one(a, b):
        return lax.dot_general(a, b, dims, preferred_element_type=F32)

    return one(lh, rh) + (one(lh, rl) + one(ll, rh))


def transform_kernel(mode_ref, t_ref, a_ref, b_ref, z_ref, th, tl, bh, bl, hh, hl):
    mode = mode_ref[0]

    @pl.loop(0, VIRT // CHUNK)
    def _(i):
        rows = pl.ds(pl.multiple_of(i * CHUNK, CHUNK), CHUNK)
        th[rows, :], tl[rows, :] = halves(t_ref[rows, :])
        bh[rows, :], bl[rows, :] = halves(b_ref[rows, :])

    @pl.loop(0, VIRT // CHUNK)
    def _(i):
        rows = pl.ds(pl.multiple_of(i * CHUNK, CHUNK), CHUNK)
        ah, al = halves(a_ref[rows, :])
        hh[rows, :], hl[rows, :] = halves(dot3(ah, al, th[...], tl[...], NN))

    @pl.when(mode == 0)
    def _():
        @pl.loop(0, VIRT // CHUNK)
        def _(i):
            rows = pl.ds(pl.multiple_of(i * CHUNK, CHUNK), CHUNK)
            z_ref[rows, :] = dot3(bh[rows, :], bl[rows, :], hh[...], hl[...], NT)

    @pl.when(mode != 0)
    def _():
        @pl.loop(0, VIRT // CHUNK)
        def _(i):
            rows = pl.ds(pl.multiple_of(i * CHUNK, CHUNK), CHUNK)
            z_ref[rows, :] = dot3(hh[rows, :], hl[rows, :], bh[...], bl[...], NT)

    @pl.when(mode == 2)
    def _():
        @pl.loop(0, VIRT // CHUNK)
        def _(i):
            rows = pl.ds(pl.multiple_of(i * CHUNK, CHUNK), CHUNK)
            other = dot3(bh[rows, :], bl[rows, :], hh[...], hl[...], NT)
            z_ref[rows, :] = 0.5 * (z_ref[rows, :] + other)


def transform(mode, t, a, b):
    vmem = pl.BlockSpec(memory_space=pltpu.VMEM)
    return pl.pallas_call(
        transform_kernel,
        out_shape=jax.ShapeDtypeStruct((VIRT, VIRT), F32),
        in_specs=[pl.BlockSpec(memory_space=pltpu.SMEM), vmem, vmem, vmem],
        out_specs=vmem,
        scratch_shapes=[pltpu.VMEM((VIRT, VIRT), BF16)] * 6,
        compiler_params=pltpu.CompilerParams(vmem_limit_bytes=40 * 2**20),
        name="transform",
    )(mode, t, a, b)


LOST = (
    [(p0, 7, q0) for p0 in range(2) for q0 in range(2)]
    + [(p0, 6, q0) for p0 in range(2) for q0 in range(2)]
    + [(p0, 5, q0) for p0 in range(2) for q0 in range(2)]
    + [(1, 0, 0), (0, 4, 1), (0, 4, 0), (1, 4, 1)]
)


def item(z_ref, got, row, p0, step, q0):
    own = z_ref[p0, lax.rem(row + step, ROWS), q0]
    if step == 0:
        return own + z_ref[q0, row, p0]
    return own + got[step][q0, p0]


def lost_kernel(row_ref, z_ref, g7, g6, g5, g4, o_ref, stage):
    row = row_ref[0]
    got = {7: g7, 6: g6, 5: g5, 4: g4}
    for n, (p0, step, q0) in enumerate(LOST):
        stage[n * WIDTH : (n + 1) * WIDTH, :] = item(z_ref, got, row, p0, step, q0)
    for i in range(HALF // 128):
        o_ref[:, i * 128 : (i + 1) * 128] = stage[i * 128 : (i + 1) * 128, :].T


def lost_items(row, z, g7, g6, g5, g4):
    vmem = pl.BlockSpec(memory_space=pltpu.VMEM)
    return pl.pallas_call(
        lost_kernel,
        out_shape=jax.ShapeDtypeStruct((VIRT, HALF), F32),
        in_specs=[pl.BlockSpec(memory_space=pltpu.SMEM)] + [vmem] * 5,
        out_specs=vmem,
        scratch_shapes=[pltpu.VMEM((HALF, VIRT), F32)],
        compiler_params=pltpu.CompilerParams(vmem_limit_bytes=40 * 2**20),
        name="lost_items",
    )(row, z, g7, g6, g5, g4)


def finish_kernel(row_ref, z_ref, g4, g3, g2, g1, back_ref, w_ref, d_ref, o_ref, tiles, s_ref):
    row = row_ref[0]
    got = {4: g4, 3: g3, 2: g2, 1: g1}
    group = lax.broadcasted_iota(jnp.int32, (WIDTH, HALF), 1) // WIDTH
    for bit in (1, 2, 4, 8):
        upper = (group // bit) % 2 == 1
        for half in range(2):
            for c in range(16):
                if c & bit:
                    continue
                if bit == 1:
                    low = back_ref[half * 16 + c]
                    high = back_ref[half * 16 + c + bit]
                else:
                    low = tiles[half, c]
                    high = tiles[half, c + bit]
                tiles[half, c] = jnp.where(upper, pltpu.roll(high, bit * WIDTH, 1), low)
                tiles[half, c + bit] = jnp.where(upper, high, pltpu.roll(low, HALF - bit * WIDTH, 1))
    place = {key: n for n, key in enumerate(LOST)}
    for p0 in range(2):
        for step in range(ROWS):
            for q0 in range(2):
                n = step * 2 + q0
                key = (p0, step, q0)
                tie = step == 4 and p0 == q0
                if key not in place or tie:
                    kept = item(z_ref, got, row, p0, step, q0)
                for half in range(2):
                    lanes = slice(half * HALF, (half + 1) * HALF)
                    if key not in place:
                        s_ref[p0, n, :, lanes] = kept[:, lanes]
                    elif tie:
                        s_ref[p0, n, :, lanes] = jnp.where(
                            row < ROWS // 2, kept[:, lanes], tiles[half, place[key]]
                        )
                    else:
                        s_ref[p0, n, :, lanes] = tiles[half, place[key]]
    wh, wl = halves(w_ref[...])
    for p0 in range(2):
        for g in range(WIDTH // 8):
            rows = slice(g * 8, (g + 1) * 8)
            sh, sl = halves(s_ref[p0, :, rows, :].reshape(OCC * 8, VIRT))
            total = dot3(wh, wl, sh, sl, NN).reshape(OCC, 8, VIRT)
            o_ref[p0, :, rows, :] = total / d_ref[p0, :, rows, :]


def finish(row, z, g4, g3, g2, g1, back, w, d):
    vmem = pl.BlockSpec(memory_space=pltpu.VMEM)
    return pl.pallas_call(
        finish_kernel,
        out_shape=jax.ShapeDtypeStruct(d.shape, F32),
        in_specs=[pl.BlockSpec(memory_space=pltpu.SMEM)] + [vmem] * 8,
        out_specs=vmem,
        scratch_shapes=[
            pltpu.VMEM((2, OCC, WIDTH, HALF), F32),
            pltpu.VMEM((2, OCC, WIDTH, VIRT), F32),
        ],
        compiler_params=pltpu.CompilerParams(vmem_limit_bytes=48 * 2**20),
        name="finish",
    )(row, z, g4, g3, g2, g1, back, w, d)


def on_device(amplitudes, first_rotation, second_rotation, pair_weights, denominators):
    row = lax.axis_index("occi")
    column = lax.axis_index("occj")
    p = 2 * row + column // OCC
    ahead = jnp.mod(column % OCC - p, OCC)
    wins = ((ahead >= 1) & (ahead <= 7)) | ((ahead == 8) & (p < 8))
    mode = jnp.where(ahead == 0, 2, jnp.where(wins, 0, 1)).astype(jnp.int32).reshape(1)
    row_here = row.astype(jnp.int32).reshape(1)

    turned = jnp.roll(pair_weights, -2 * row, axis=0)
    spread = jnp.einsum("jk,xy->kxjy", turned, jnp.eye(8, dtype=F32), precision="highest").reshape(128, 128)

    z = transform(mode, amplitudes[0], first_rotation, second_rotation)
    z = lax.all_to_all(z.reshape(COLS, WIDTH, VIRT), "occj", split_axis=0, concat_axis=0, tiled=True)
    z = z.reshape(2, ROWS, 2, WIDTH, VIRT)

    def exchange(step):
        out = lax.dynamic_index_in_dim(z, jnp.mod(row + step, ROWS), 1, keepdims=False)
        return lax.ppermute(out, "occi", [(r, (r + step) % ROWS) for r in range(ROWS)])

    got = {ROWS - step: exchange(step) for step in range(1, ROWS)}
    lost = lost_items(row_here, z, got[7], got[6], got[5], got[4])
    back = lax.all_to_all(lost.reshape(COLS, WIDTH, HALF), "occj", split_axis=0, concat_axis=0, tiled=True)
    return finish(row_here, z, got[4], got[3], got[2], got[1], back, spread, denominators)


def solution(mesh):
    placed = (P(("occi", "occj"), None, None), P(), P(), P(), P("occi", None, "occj", None))
    return jax.shard_map(
        on_device,
        mesh=mesh,
        in_specs=placed,
        out_specs=P("occi", None, "occj", None),
        check_vma=False,
    )
```

```python
import jax
import jax.numpy as jnp
from jax import lax
from jax.experimental import pallas as pl
from jax.experimental.pallas import tpu as pltpu
from jax.sharding import PartitionSpec as P

OCC = 16
VIRT = 768
ROWS = 8
COLS = 32
WIDTH = VIRT // COLS
HALF = VIRT // 2
CHUNK = 256
PARTS = VIRT // CHUNK
KEPT = 9
LOST = 8
F32 = jnp.float32
BF16 = jnp.bfloat16
NT = (((1,), (1,)), ((), ()))
NN = (((1,), (0,)), ((), ()))
HBM = pl.BlockSpec(memory_space=pltpu.HBM)
VMEM = pl.BlockSpec(memory_space=pltpu.VMEM)
SMEM = pl.BlockSpec(memory_space=pltpu.SMEM)


def halves(x):
    high = x.astype(BF16)
    return high, (x - high.astype(F32)).astype(BF16)


def dot3(lh, ll, rh, rl, dims):
    def one(a, b):
        return lax.dot_general(a, b, dims, preferred_element_type=F32)

    return one(lh, rh) + (one(lh, rl) + one(ll, rh))


def transform_kernel(mode_ref, t_ref, a_ref, b_ref, z_ref, t, a, b, z, th, tl, high, low, ins, outs):
    mode = mode_ref[0]
    mine = jnp.where(mode == 0, 1, 0)
    chunks = [slice(i * CHUNK, (i + 1) * CHUNK) for i in range(PARTS)]
    copies = []
    for n, (src, dst) in enumerate(((t_ref, t), (a_ref, a), (b_ref, b))):
        copies.append([pltpu.make_async_copy(src.at[r], dst.at[r], ins.at[n, i]) for i, r in enumerate(chunks)])
        for copy in copies[-1]:
            copy.start()
    for copy, r in zip(copies[0], chunks):
        copy.wait()
        th[r, :], tl[r, :] = halves(t[r, :])
    for copy, r in zip(copies[1], chunks):
        copy.wait()
        ah, al = halves(a[r, :])
        high[mine, r, :], low[mine, r, :] = halves(dot3(ah, al, th[...], tl[...], NN))
    for copy, r in zip(copies[2], chunks):
        copy.wait()
        high[1 - mine, r, :], low[1 - mine, r, :] = halves(b[r, :])
    sends = [pltpu.make_async_copy(z.at[r], z_ref.at[r], outs.at[i]) for i, r in enumerate(chunks)]
    for send, r in zip(sends, chunks):
        z[r, :] = dot3(high[0, r, :], low[0, r, :], high[1], low[1], NT)

        @pl.when(mode != 2)
        def _():
            send.start()

    @pl.when(mode == 2)
    def _():
        tiles = [slice(i * 128, (i + 1) * 128) for i in range(VIRT // 128)]
        for n, i in enumerate(tiles):
            for j in tiles[n:]:
                mean = 0.5 * (z[i, j] + z[j, i].T)
                z[i, j] = mean
                if i != j:
                    z[j, i] = mean.T
        for send in sends:
            send.start()

    for send in sends:
        send.wait()


def transform(mode, t, a, b):
    return pl.pallas_call(
        transform_kernel,
        out_shape=jax.ShapeDtypeStruct((VIRT, VIRT), F32),
        in_specs=[SMEM, HBM, HBM, HBM],
        out_specs=HBM,
        scratch_shapes=[pltpu.VMEM((VIRT, VIRT), F32)] * 4
        + [pltpu.VMEM((VIRT, VIRT), BF16)] * 2
        + [pltpu.VMEM((2, VIRT, VIRT), BF16)] * 2
        + [pltpu.SemaphoreType.DMA((3, PARTS)), pltpu.SemaphoreType.DMA((PARTS,))],
        compiler_params=pltpu.CompilerParams(vmem_limit_bytes=63_500_000),
        name="transform",
    )(mode, t, a, b)


def lost_kernel(row_ref, z_hbm, e_hbm, o_ref, own, other, stage, turned, ins, outs):
    row = row_ref[0]
    loads = []
    for n in range(2 * LOST):
        p0, m = divmod(n, LOST)
        partner = 8 + p0 + m
        there = lax.rem(row + (partner // 2) % ROWS, ROWS)
        loads.append(
            (
                pltpu.make_async_copy(z_hbm.at[p0, there, partner % 2], own.at[n], ins.at[0, n]),
                pltpu.make_async_copy(e_hbm.at[there, partner % 2, p0], other.at[n], ins.at[1, n]),
            )
        )
        for load in loads[-1]:
            load.start()
    for n, pair in enumerate(loads):
        for load in pair:
            load.wait()
        stage[n * WIDTH : (n + 1) * WIDTH, :] = own[n] + other[n]
    sends = []
    for i in range(VIRT // CHUNK):
        rows = slice(i * CHUNK, (i + 1) * CHUNK)
        turned[rows, :] = stage[:, rows].T
        sends.append(pltpu.make_async_copy(turned.at[rows], o_ref.at[rows], outs.at[i]))
        sends[-1].start()
    for send in sends:
        send.wait()


def lost_items(row, z, e):
    return pl.pallas_call(
        lost_kernel,
        out_shape=jax.ShapeDtypeStruct((VIRT, HALF), F32),
        in_specs=[SMEM, HBM, HBM],
        out_specs=HBM,
        scratch_shapes=[
            pltpu.VMEM((2 * LOST, WIDTH, VIRT), F32),
            pltpu.VMEM((2 * LOST, WIDTH, VIRT), F32),
            pltpu.VMEM((HALF, VIRT), F32),
            pltpu.VMEM((VIRT, HALF), F32),
            pltpu.SemaphoreType.DMA((2, 2 * LOST)),
            pltpu.SemaphoreType.DMA((PARTS,)),
        ],
        compiler_params=pltpu.CompilerParams(vmem_limit_bytes=63_500_000),
        name="lost_items",
    )(row, z, e)


def weights(w_ref, row, first, many, tie, count):
    def iota(shape, dim):
        return lax.broadcasted_iota(jnp.int32, shape, dim)

    out = OCC * 8
    pick = (iota((out, OCC), 0) // 8 == iota((out, OCC), 1)).astype(F32)
    m = iota((OCC, many * 8), 1) // 8
    index = (m + (first + 2 * row)) % OCC
    chosen = jnp.where(iota((OCC, many * 8), 0) == index, jnp.where(m == tie, count, 1.0), 0.0)
    full = lax.dot_general(pick, w_ref[...], NT, precision=lax.Precision.HIGHEST, preferred_element_type=F32)
    full = lax.dot_general(full, chosen, NN, precision=lax.Precision.HIGHEST, preferred_element_type=F32)
    same = iota((out, many * 8), 0) % 8 == iota((out, many * 8), 1) % 8
    return halves(jnp.where(same, full, 0.0))


def kept_kernel(row_ref, z_ref, e_ref, w_ref, d_ref, u_ref, r_ref):
    row = row_ref[0]
    count = jnp.where(row < ROWS // 2, 1.0, 0.0)
    for p0 in range(2):
        wh, wl = weights(w_ref, row, p0, KEPT, KEPT - 1, count)
        for g in range(WIDTH // 8):
            rows = slice(g * 8, (g + 1) * 8)
            there = [lax.rem(row + n // 2, ROWS) for n in range(p0, p0 + KEPT)]
            parts = [
                z_ref[p0, t, n % 2, rows, :] + e_ref[t, n % 2, p0, rows, :]
                for t, n in zip(there, range(p0, p0 + KEPT))
            ]
            sh, sl = halves(jnp.concatenate(parts, axis=0))
            total = dot3(wh, wl, sh, sl, NN).reshape(OCC, 8, VIRT)
            scale = 1.0 / d_ref[p0, :, rows, :]
            r_ref[p0, :, rows, :] = scale
            u_ref[p0, :, rows, :] = total * scale


def kept_items(row, z, e, w, d):
    shape = jax.ShapeDtypeStruct(d.shape, F32)
    return pl.pallas_call(
        kept_kernel,
        out_shape=(shape, shape),
        in_specs=[SMEM] + [VMEM] * 4,
        out_specs=(VMEM, VMEM),
        compiler_params=pltpu.CompilerParams(vmem_limit_bytes=40 * 2**20),
        cost_estimate=pl.CostEstimate(flops=2 * 10**9, bytes_accessed=12 * 10**6, transcendentals=0),
        name="kept_items",
    )(row, z, e, w, d)


def finish_kernel(row_ref, back_ref, w_ref, u_hbm, r_hbm, o_ref, tiles, out, u_ref, r_ref, ins, outs):
    row = row_ref[0]
    loads = []
    for p0 in range(2):
        pairs = ((u_hbm, u_ref), (r_hbm, r_ref))
        loads.append([pltpu.make_async_copy(src.at[p0], dst.at[p0], ins.at[n, p0]) for n, (src, dst) in enumerate(pairs)])
    for pair in loads:
        for load in pair:
            load.start()
    group = lax.broadcasted_iota(jnp.int32, (WIDTH, HALF), 1) // WIDTH
    for bit in (1, 2, 4, 8):
        upper = (group // bit) % 2 == 1
        for half in range(2):
            for c in range(16):
                if c & bit:
                    continue
                if bit == 1:
                    low = back_ref[half * 16 + c]
                    high = back_ref[half * 16 + c + bit]
                else:
                    low = tiles[half, c]
                    high = tiles[half, c + bit]
                tiles[half, c] = jnp.where(upper, pltpu.roll(high, bit * WIDTH, 1), low)
                tiles[half, c + bit] = jnp.where(upper, high, pltpu.roll(low, HALF - bit * WIDTH, 1))
    count = jnp.where(row < ROWS // 2, 0.0, 1.0)
    sends = []
    for p0 in range(2):
        wh, wl = weights(w_ref, row, 8 + p0, LOST, 0, count)
        for load in loads[p0]:
            load.wait()
        for g in range(WIDTH // 8):
            rows = slice(g * 8, (g + 1) * 8)
            for half in range(2):
                lanes = slice(half * HALF, (half + 1) * HALF)
                sh, sl = halves(tiles[half, p0 * LOST : (p0 + 1) * LOST, rows, :].reshape(LOST * 8, HALF))
                total = dot3(wh, wl, sh, sl, NN).reshape(OCC, 8, HALF)
                out[p0, :, rows, lanes] = u_ref[p0, :, rows, lanes] + total * r_ref[p0, :, rows, lanes]
            sends.append(pltpu.make_async_copy(out.at[p0, :, rows], o_ref.at[p0, :, rows], outs.at[p0, g]))
            sends[-1].start()
    for send in sends:
        send.wait()


def finish(row, back, w, u, r):
    return pl.pallas_call(
        finish_kernel,
        out_shape=jax.ShapeDtypeStruct(u.shape, F32),
        in_specs=[SMEM, VMEM, VMEM, HBM, HBM],
        out_specs=HBM,
        scratch_shapes=[
            pltpu.VMEM((2, OCC, WIDTH, HALF), F32),
            pltpu.VMEM(u.shape, F32),
            pltpu.VMEM(u.shape, F32),
            pltpu.VMEM(u.shape, F32),
            pltpu.SemaphoreType.DMA((2, 2)),
            pltpu.SemaphoreType.DMA((2, WIDTH // 8)),
        ],
        compiler_params=pltpu.CompilerParams(vmem_limit_bytes=62_500_000),
        name="finish",
    )(row, back, w, u, r)


def on_device(amplitudes, first_rotation, second_rotation, pair_weights, denominators):
    row = lax.axis_index("occi")
    column = lax.axis_index("occj")
    p = 2 * row + column // OCC
    ahead = jnp.mod(column % OCC - p, OCC)
    wins = ((ahead >= 1) & (ahead <= 7)) | ((ahead == 8) & (p < 8))
    mode = jnp.where(ahead == 0, 2, jnp.where(wins, 0, 1)).astype(jnp.int32).reshape(1)
    row_here = row.astype(jnp.int32).reshape(1)

    z = transform(mode, amplitudes[0], first_rotation, second_rotation)
    z = lax.all_to_all(z.reshape(COLS, WIDTH, VIRT), "occj", split_axis=0, concat_axis=0, tiled=True)
    z = z.reshape(2, ROWS, 2, WIDTH, VIRT)
    e = lax.all_to_all(jnp.swapaxes(z, 0, 1), "occi", split_axis=0, concat_axis=0, tiled=True)
    lost = lost_items(row_here, z, e)
    back = lax.all_to_all(lost.reshape(COLS, WIDTH, HALF), "occj", split_axis=0, concat_axis=0, tiled=True)
    u, r = kept_items(row_here, z, e, pair_weights, denominators)
    return finish(row_here, back, pair_weights, u, r)


def solution(mesh):
    placed = (P(("occi", "occj"), None, None), P(), P(), P(), P("occi", None, "occj", None))
    return jax.shard_map(
        on_device,
        mesh=mesh,
        in_specs=placed,
        out_specs=P("occi", None, "occj", None),
        check_vma=False,
    )
```

```python
import jax
import jax.numpy as jnp
from jax import lax
from jax.experimental import pallas as pl
from jax.experimental.pallas import tpu as pltpu
from jax.sharding import PartitionSpec as P

OCC = 16
VIRT = 768
ROWS = 8
COLS = 32
WIDTH = VIRT // COLS
HALF = VIRT // 2
CHUNK = 256
PARTS = VIRT // CHUNK
KEPT = 9
LOST = 8
F32 = jnp.float32
BF16 = jnp.bfloat16
NT = (((1,), (1,)), ((), ()))
NN = (((1,), (0,)), ((), ()))
HBM = pl.BlockSpec(memory_space=pltpu.HBM)
VMEM = pl.BlockSpec(memory_space=pltpu.VMEM)
SMEM = pl.BlockSpec(memory_space=pltpu.SMEM)


def halves(x):
    high = x.astype(BF16)
    return high, (x - high.astype(F32)).astype(BF16)


def dot3(lh, ll, rh, rl, dims):
    def one(a, b):
        return lax.dot_general(a, b, dims, preferred_element_type=F32)

    return one(lh, rh) + (one(lh, rl) + one(ll, rh))


def transform_kernel(mode_ref, t_ref, a_ref, b_ref, z_ref, t, a, b, z, t3, a3, pair, ins, outs):
    mode = mode_ref[0]
    mine = jnp.where(mode == 0, 1, 0)
    chunks = [slice(i * CHUNK, (i + 1) * CHUNK) for i in range(PARTS)]
    thirds = [slice(i * VIRT, (i + 1) * VIRT) for i in range(3)]
    loads = []
    for n, (src, dst) in enumerate(((t_ref, t), (a_ref, a), (b_ref, b))):
        loads.append([pltpu.make_async_copy(src.at[r], dst.at[r], ins.at[n, i]) for i, r in enumerate(chunks)])
    for load in loads[0] + loads[1]:
        load.start()

    def put(slot, rows, x, right):
        h, l = halves(x)
        pair[slot, rows, thirds[0]] = h
        pair[slot, rows, thirds[1]] = jnp.where(right, l, h)
        pair[slot, rows, thirds[2]] = jnp.where(right, h, l)

    for i, (load, r) in enumerate(zip(loads[0], chunks)):
        load.wait()
        h, l = halves(t[r, :])
        for n, x in enumerate((h, l, h)):
            t3[n * VIRT + i * CHUNK : n * VIRT + (i + 1) * CHUNK, :] = x
    for load in loads[2]:
        load.start()
    for load, r in zip(loads[1], chunks):
        load.wait()
        h, l = halves(a[r, :])
        for third, x in zip(thirds, (h, h, l)):
            a3[r, third] = x
        put(mine, r, lax.dot_general(a3[r, :], t3[...], NN, preferred_element_type=F32), mode == 0)
    for load, r in zip(loads[2], chunks):
        load.wait()
        put(1 - mine, r, b[r, :], mode != 0)
    sends = [pltpu.make_async_copy(z.at[r], z_ref.at[r], outs.at[i]) for i, r in enumerate(chunks)]
    for send, r in zip(sends, chunks):
        z[r, :] = lax.dot_general(pair[0, r, :], pair[1], NT, preferred_element_type=F32)

        @pl.when(mode != 2)
        def _():
            send.start()

    @pl.when(mode == 2)
    def _():
        tiles = [slice(i * 128, (i + 1) * 128) for i in range(VIRT // 128)]
        for n, i in enumerate(tiles):
            for j in tiles[n:]:
                mean = 0.5 * (z[i, j] + z[j, i].T)
                z[i, j] = mean
                if i != j:
                    z[j, i] = mean.T
        for send in sends:
            send.start()

    for send in sends:
        send.wait()


def transform(mode, t, a, b):
    return pl.pallas_call(
        transform_kernel,
        out_shape=jax.ShapeDtypeStruct((VIRT, VIRT), F32),
        in_specs=[SMEM, HBM, HBM, HBM],
        out_specs=HBM,
        scratch_shapes=[pltpu.VMEM((VIRT, VIRT), F32)] * 4
        + [pltpu.VMEM((3 * VIRT, VIRT), BF16), pltpu.VMEM((VIRT, 3 * VIRT), BF16), pltpu.VMEM((2, VIRT, 3 * VIRT), BF16)]
        + [pltpu.SemaphoreType.DMA((3, PARTS)), pltpu.SemaphoreType.DMA((PARTS,))],
        compiler_params=pltpu.CompilerParams(vmem_limit_bytes=63_500_000),
        name="transform",
    )(mode, t, a, b)


STEPS = (4, 5, 6, 7, 0)


def lost_kernel(row_ref, z_hbm, e_hbm, o_ref, own, other, stage, turned, ins, outs):
    row = row_ref[0]
    loads = []
    for i, step in enumerate(STEPS[:4]):
        there = lax.rem(row + step, ROWS)
        loads.append(
            [pltpu.make_async_copy(z_hbm.at[p0, there], own.at[p0, i], ins.at[i, p0]) for p0 in range(2)]
            + [pltpu.make_async_copy(e_hbm.at[there], other.at[i], ins.at[i, 2])]
        )
    loads.append([pltpu.make_async_copy(z_hbm.at[p0, row, 1 - p0], own.at[p0, 4, 1 - p0], ins.at[4, p0]) for p0 in range(2)])
    for group in loads:
        for load in group:
            load.start()
    for i, group in enumerate(loads):
        for load in group:
            load.wait()
        for p0 in range(2):
            for m in range(LOST):
                partner = 8 + p0 + m
                if (partner // 2) % ROWS == STEPS[i]:
                    q0 = partner % 2
                    second = own[1 - p0, i, p0] if i == 4 else other[i, q0, p0]
                    at = (p0 * LOST + m) * WIDTH
                    stage[at : at + WIDTH, :] = own[p0, i, q0] + second
    sends = []
    for i in range(PARTS):
        rows = slice(i * CHUNK, (i + 1) * CHUNK)
        turned[rows, :] = stage[:, rows].T
        sends.append(pltpu.make_async_copy(turned.at[rows], o_ref.at[rows], outs.at[i]))
        sends[-1].start()
    for send in sends:
        send.wait()


def lost_items(row, z, e):
    return pl.pallas_call(
        lost_kernel,
        out_shape=jax.ShapeDtypeStruct((VIRT, HALF), F32),
        in_specs=[SMEM, HBM, HBM],
        out_specs=HBM,
        scratch_shapes=[
            pltpu.VMEM((2, 5, 2, WIDTH, VIRT), F32),
            pltpu.VMEM((4, 2, 2, WIDTH, VIRT), F32),
            pltpu.VMEM((HALF, VIRT), F32),
            pltpu.VMEM((VIRT, HALF), F32),
            pltpu.SemaphoreType.DMA((5, 3)),
            pltpu.SemaphoreType.DMA((PARTS,)),
        ],
        compiler_params=pltpu.CompilerParams(vmem_limit_bytes=63_500_000),
        name="lost_items",
    )(row, z, e)


def weights(w_ref, row, first, many, tie, count):
    def iota(shape, dim):
        return lax.broadcasted_iota(jnp.int32, shape, dim)

    out = OCC * 8
    pick = (iota((out, OCC), 0) // 8 == iota((out, OCC), 1)).astype(F32)
    m = iota((OCC, many * 8), 1) // 8
    index = (m + (first + 2 * row)) % OCC
    chosen = jnp.where(iota((OCC, many * 8), 0) == index, jnp.where(m == tie, count, 1.0), 0.0)
    full = lax.dot_general(pick, w_ref[...], NT, precision=lax.Precision.HIGHEST, preferred_element_type=F32)
    full = lax.dot_general(full, chosen, NN, precision=lax.Precision.HIGHEST, preferred_element_type=F32)
    same = iota((out, many * 8), 0) % 8 == iota((out, many * 8), 1) % 8
    return halves(jnp.where(same, full, 0.0))


def kept_kernel(row_ref, z_ref, e_ref, w_ref, d_ref, u_ref, r_ref):
    row = row_ref[0]
    count = jnp.where(row < ROWS // 2, 1.0, 0.0)
    for p0 in range(2):
        wh, wl = weights(w_ref, row, p0, KEPT, KEPT - 1, count)
        for g in range(WIDTH // 8):
            rows = slice(g * 8, (g + 1) * 8)
            there = [lax.rem(row + n // 2, ROWS) for n in range(p0, p0 + KEPT)]
            parts = [
                z_ref[p0, t, n % 2, rows, :] + e_ref[t, n % 2, p0, rows, :]
                for t, n in zip(there, range(p0, p0 + KEPT))
            ]
            sh, sl = halves(jnp.concatenate(parts, axis=0))
            total = dot3(wh, wl, sh, sl, NN).reshape(OCC, 8, VIRT)
            scale = 1.0 / d_ref[p0, :, rows, :]
            r_ref[p0, :, rows, :] = scale
            u_ref[p0, :, rows, :] = total * scale


def kept_items(row, z, e, w, d):
    shape = jax.ShapeDtypeStruct(d.shape, F32)
    return pl.pallas_call(
        kept_kernel,
        out_shape=(shape, shape),
        in_specs=[SMEM] + [VMEM] * 4,
        out_specs=(VMEM, VMEM),
        compiler_params=pltpu.CompilerParams(vmem_limit_bytes=40 * 2**20),
        cost_estimate=pl.CostEstimate(flops=2 * 10**9, bytes_accessed=12 * 10**6, transcendentals=0),
        name="kept_items",
    )(row, z, e, w, d)


def finish_kernel(row_ref, back_hbm, w_ref, u_hbm, r_hbm, o_ref, back, u, r, out, ins, outs):
    row = row_ref[0]
    groups = [slice(g * 8, (g + 1) * 8) for g in range(WIDTH // 8)]
    loads = []
    for g, rows in enumerate(groups):
        loads.append(
            [
                pltpu.make_async_copy(back_hbm.at[:, rows], back.at[:, rows], ins.at[0, g]),
                pltpu.make_async_copy(u_hbm.at[:, :, rows], u.at[:, :, rows], ins.at[1, g]),
                pltpu.make_async_copy(r_hbm.at[:, :, rows], r.at[:, :, rows], ins.at[2, g]),
            ]
        )
        for load in loads[-1]:
            load.start()
    count = jnp.where(row < ROWS // 2, 0.0, 1.0)
    spread = []
    for p0 in range(2):
        wh, wl = weights(w_ref, row, 8 + p0, LOST, 0, count)
        spread.append(jnp.concatenate([wh, wh, wl], axis=1))
    group = lax.broadcasted_iota(jnp.int32, (8, HALF), 1) // WIDTH
    sends = []
    for g, rows in enumerate(groups):
        loads[g][0].wait()
        for half in range(2):
            lanes = slice(half * HALF, (half + 1) * HALF)
            x = [back[half * 16 + c, rows, :] for c in range(16)]
            for bit in (1, 2, 4, 8):
                upper = (group // bit) % 2 == 1
                for c in range(16):
                    if not c & bit:
                        low, high = x[c], x[c + bit]
                        x[c] = jnp.where(upper, pltpu.roll(high, bit * WIDTH, 1), low)
                        x[c + bit] = jnp.where(upper, high, pltpu.roll(low, HALF - bit * WIDTH, 1))
            if half == 0:
                for load in loads[g][1:]:
                    load.wait()
            for p0 in range(2):
                sh, sl = halves(jnp.concatenate(x[p0 * LOST : (p0 + 1) * LOST], axis=0))
                stacked = jnp.concatenate([sh, sl, sh], axis=0)
                total = lax.dot_general(spread[p0], stacked, NN, preferred_element_type=F32)
                total = total.reshape(OCC, 8, HALF)
                out[p0, :, rows, lanes] = u[p0, :, rows, lanes] + total * r[p0, :, rows, lanes]
        sends.append(pltpu.make_async_copy(out.at[:, :, rows], o_ref.at[:, :, rows], outs.at[g]))
        sends[-1].start()
    for send in sends:
        send.wait()


def finish(row, back, w, u, r):
    return pl.pallas_call(
        finish_kernel,
        out_shape=jax.ShapeDtypeStruct(u.shape, F32),
        in_specs=[SMEM, HBM, VMEM, HBM, HBM],
        out_specs=HBM,
        scratch_shapes=[pltpu.VMEM(back.shape, F32)]
        + [pltpu.VMEM(u.shape, F32)] * 3
        + [pltpu.SemaphoreType.DMA((3, WIDTH // 8)), pltpu.SemaphoreType.DMA((WIDTH // 8,))],
        compiler_params=pltpu.CompilerParams(vmem_limit_bytes=62_500_000),
        name="finish",
    )(row, back, w, u, r)


def on_device(amplitudes, first_rotation, second_rotation, pair_weights, denominators):
    row = lax.axis_index("occi")
    column = lax.axis_index("occj")
    p = 2 * row + column // OCC
    ahead = jnp.mod(column % OCC - p, OCC)
    wins = ((ahead >= 1) & (ahead <= 7)) | ((ahead == 8) & (p < 8))
    mode = jnp.where(ahead == 0, 2, jnp.where(wins, 0, 1)).astype(jnp.int32).reshape(1)
    row_here = row.astype(jnp.int32).reshape(1)

    z = transform(mode, amplitudes[0], first_rotation, second_rotation)
    z = lax.all_to_all(z.reshape(COLS, WIDTH, VIRT), "occj", split_axis=0, concat_axis=0, tiled=True)
    z = z.reshape(2, ROWS, 2, WIDTH, VIRT)
    e = lax.all_to_all(jnp.swapaxes(z, 0, 1), "occi", split_axis=0, concat_axis=0, tiled=True)
    lost = lost_items(row_here, z, e)
    back = lax.all_to_all(lost.reshape(COLS, WIDTH, HALF), "occj", split_axis=0, concat_axis=0, tiled=True)
    u, r = kept_items(row_here, z, e, pair_weights, denominators)
    return finish(row_here, back, pair_weights, u, r)


def solution(mesh):
    placed = (P(("occi", "occj"), None, None), P(), P(), P(), P("occi", None, "occj", None))
    return jax.shard_map(
        on_device,
        mesh=mesh,
        in_specs=placed,
        out_specs=P("occi", None, "occj", None),
        check_vma=False,
    )
```

```python
import jax
import jax.numpy as jnp
from jax import lax
from jax.experimental import pallas as pl
from jax.experimental.pallas import tpu as pltpu
from jax.sharding import PartitionSpec as P

OCC = 16
VIRT = 768
ROWS = 8
COLS = 32
WIDTH = VIRT // COLS
HALF = VIRT // 2
CHUNK = 256
PARTS = VIRT // CHUNK
KEPT = 9
LOST = 8
F32 = jnp.float32
BF16 = jnp.bfloat16
NT = (((1,), (1,)), ((), ()))
NN = (((1,), (0,)), ((), ()))
HBM = pl.BlockSpec(memory_space=pltpu.HBM)
VMEM = pl.BlockSpec(memory_space=pltpu.VMEM)
SMEM = pl.BlockSpec(memory_space=pltpu.SMEM)


def halves(x):
    high = x.astype(BF16)
    return high, (x - high.astype(F32)).astype(BF16)


def dot3(lh, ll, rh, rl, dims):
    def one(a, b):
        return lax.dot_general(a, b, dims, preferred_element_type=F32)

    return one(lh, rh) + (one(lh, rl) + one(ll, rh))


def transform_kernel(mode_ref, t_ref, a_ref, b_ref, z_ref, t, a, b, z, t3, a3, pair, ins, outs):
    mode = mode_ref[0]
    mine = jnp.where(mode == 0, 1, 0)
    chunks = [slice(i * CHUNK, (i + 1) * CHUNK) for i in range(PARTS)]
    thirds = [slice(i * VIRT, (i + 1) * VIRT) for i in range(3)]
    loads = []
    for n, (src, dst) in enumerate(((t_ref, t), (a_ref, a), (b_ref, b))):
        loads.append([pltpu.make_async_copy(src.at[r], dst.at[r], ins.at[n, i]) for i, r in enumerate(chunks)])
    for load in loads[0] + loads[1]:
        load.start()

    def put(slot, rows, x, right):
        h, l = halves(x)
        pair[slot, rows, thirds[0]] = h
        pair[slot, rows, thirds[1]] = jnp.where(right, l, h)
        pair[slot, rows, thirds[2]] = jnp.where(right, h, l)

    for i, (load, r) in enumerate(zip(loads[0], chunks)):
        load.wait()
        h, l = halves(t[r, :])
        for n, x in enumerate((h, l, h)):
            t3[n * VIRT + i * CHUNK : n * VIRT + (i + 1) * CHUNK, :] = x
    for load in loads[2]:
        load.start()
    for load, r in zip(loads[1], chunks):
        load.wait()
        h, l = halves(a[r, :])
        for third, x in zip(thirds, (h, h, l)):
            a3[r, third] = x
        put(mine, r, lax.dot_general(a3[r, :], t3[...], NN, preferred_element_type=F32), mode == 0)
    for load, r in zip(loads[2], chunks):
        load.wait()
        put(1 - mine, r, b[r, :], mode != 0)
    sends = [pltpu.make_async_copy(z.at[r], z_ref.at[r], outs.at[i]) for i, r in enumerate(chunks)]
    for send, r in zip(sends, chunks):
        z[r, :] = lax.dot_general(pair[0, r, :], pair[1], NT, preferred_element_type=F32)

        @pl.when(mode != 2)
        def _():
            send.start()

    @pl.when(mode == 2)
    def _():
        tiles = [slice(i * 128, (i + 1) * 128) for i in range(VIRT // 128)]
        for n, i in enumerate(tiles):
            for j in tiles[n:]:
                mean = 0.5 * (z[i, j] + z[j, i].T)
                z[i, j] = mean
                if i != j:
                    z[j, i] = mean.T
        for send in sends:
            send.start()

    for send in sends:
        send.wait()


def transform(mode, t, a, b):
    return pl.pallas_call(
        transform_kernel,
        out_shape=jax.ShapeDtypeStruct((VIRT, VIRT), F32),
        in_specs=[SMEM, HBM, HBM, HBM],
        out_specs=HBM,
        scratch_shapes=[pltpu.VMEM((VIRT, VIRT), F32)] * 4
        + [pltpu.VMEM((3 * VIRT, VIRT), BF16), pltpu.VMEM((VIRT, 3 * VIRT), BF16), pltpu.VMEM((2, VIRT, 3 * VIRT), BF16)]
        + [pltpu.SemaphoreType.DMA((3, PARTS)), pltpu.SemaphoreType.DMA((PARTS,))],
        compiler_params=pltpu.CompilerParams(vmem_limit_bytes=63_500_000),
        name="transform",
    )(mode, t, a, b)


STEPS = (7, 6, 5, 4, 0)


def lost_kernel(row_ref, z_hbm, g7, g6, g5, g4, o_ref, own, other, stage, turned, ins, outs):
    row = row_ref[0]
    loads = []
    for i, (step, got) in enumerate(zip(STEPS, (g7, g6, g5, g4))):
        there = lax.rem(row + step, ROWS)
        loads.append(
            [pltpu.make_async_copy(z_hbm.at[p0, there], own.at[p0, i], ins.at[i, p0]) for p0 in range(2)]
            + [pltpu.make_async_copy(got, other.at[i], ins.at[i, 2])]
        )
    loads.append([pltpu.make_async_copy(z_hbm.at[p0, row, 1 - p0], own.at[p0, 4, 1 - p0], ins.at[4, p0]) for p0 in range(2)])
    for group in loads:
        for load in group:
            load.start()
    for i, group in enumerate(loads):
        for load in group:
            load.wait()
        for p0 in range(2):
            for m in range(LOST):
                partner = 8 + p0 + m
                if (partner // 2) % ROWS == STEPS[i]:
                    q0 = partner % 2
                    second = own[1 - p0, i, p0] if i == 4 else other[i, q0, p0]
                    at = (p0 * LOST + m) * WIDTH
                    stage[at : at + WIDTH, :] = own[p0, i, q0] + second
    sends = []
    for i in range(PARTS):
        rows = slice(i * CHUNK, (i + 1) * CHUNK)
        turned[rows, :] = stage[:, rows].T
        sends.append(pltpu.make_async_copy(turned.at[rows], o_ref.at[rows], outs.at[i]))
        sends[-1].start()
    for send in sends:
        send.wait()


def lost_items(row, z, *got):
    return pl.pallas_call(
        lost_kernel,
        out_shape=jax.ShapeDtypeStruct((VIRT, HALF), F32),
        in_specs=[SMEM] + [HBM] * 5,
        out_specs=HBM,
        scratch_shapes=[
            pltpu.VMEM((2, 5, 2, WIDTH, VIRT), F32),
            pltpu.VMEM((4, 2, 2, WIDTH, VIRT), F32),
            pltpu.VMEM((HALF, VIRT), F32),
            pltpu.VMEM((VIRT, HALF), F32),
            pltpu.SemaphoreType.DMA((5, 3)),
            pltpu.SemaphoreType.DMA((PARTS,)),
        ],
        compiler_params=pltpu.CompilerParams(vmem_limit_bytes=63_500_000),
        name="lost_items",
    )(row, z, *got)


def weights(w_ref, row, first, many, tie, count):
    def iota(shape, dim):
        return lax.broadcasted_iota(jnp.int32, shape, dim)

    out = OCC * 8
    pick = (iota((out, OCC), 0) // 8 == iota((out, OCC), 1)).astype(F32)
    m = iota((OCC, many * 8), 1) // 8
    index = (m + (first + 2 * row)) % OCC
    chosen = jnp.where(iota((OCC, many * 8), 0) == index, jnp.where(m == tie, count, 1.0), 0.0)
    full = lax.dot_general(pick, w_ref[...], NT, precision=lax.Precision.HIGHEST, preferred_element_type=F32)
    full = lax.dot_general(full, chosen, NN, precision=lax.Precision.HIGHEST, preferred_element_type=F32)
    same = iota((out, many * 8), 0) % 8 == iota((out, many * 8), 1) % 8
    return halves(jnp.where(same, full, 0.0))


def kept_kernel(row_ref, z_ref, g4, g3, g2, g1, w_ref, d_ref, u_ref, r_ref):
    row = row_ref[0]
    got = {4: g4, 3: g3, 2: g2, 1: g1}
    count = jnp.where(row < ROWS // 2, 1.0, 0.0)
    for p0 in range(2):
        wh, wl = weights(w_ref, row, p0, KEPT, KEPT - 1, count)
        for g in range(WIDTH // 8):
            rows = slice(g * 8, (g + 1) * 8)
            parts = []
            for n in range(p0, p0 + KEPT):
                there, q0 = n // 2, n % 2
                first = z_ref[p0, lax.rem(row + there, ROWS), q0, rows, :]
                second = got[there][q0, p0, rows, :] if there else z_ref[q0, row, p0, rows, :]
                parts.append(first + second)
            sh, sl = halves(jnp.concatenate(parts, axis=0))
            total = dot3(wh, wl, sh, sl, NN).reshape(OCC, 8, VIRT)
            scale = 1.0 / d_ref[p0, :, rows, :]
            r_ref[p0, :, rows, :] = scale
            u_ref[p0, :, rows, :] = total * scale


def kept_items(row, z, *rest):
    shape = jax.ShapeDtypeStruct(rest[-1].shape, F32)
    return pl.pallas_call(
        kept_kernel,
        out_shape=(shape, shape),
        in_specs=[SMEM] + [VMEM] * 7,
        out_specs=(VMEM, VMEM),
        compiler_params=pltpu.CompilerParams(vmem_limit_bytes=40 * 2**20),
        cost_estimate=pl.CostEstimate(flops=10**11, bytes_accessed=12 * 10**6, transcendentals=0),
        name="kept_items",
    )(row, z, *rest)


def finish_kernel(row_ref, back_hbm, w_ref, u_hbm, r_hbm, o_ref, back, u, r, out, ins, outs):
    row = row_ref[0]
    groups = [slice(g * 8, (g + 1) * 8) for g in range(WIDTH // 8)]
    loads = []
    for g, rows in enumerate(groups):
        loads.append(
            [
                pltpu.make_async_copy(back_hbm.at[:, rows], back.at[:, rows], ins.at[0, g]),
                pltpu.make_async_copy(u_hbm.at[:, :, rows], u.at[:, :, rows], ins.at[1, g]),
                pltpu.make_async_copy(r_hbm.at[:, :, rows], r.at[:, :, rows], ins.at[2, g]),
            ]
        )
        for load in loads[-1]:
            load.start()
    count = jnp.where(row < ROWS // 2, 0.0, 1.0)
    spread = []
    for p0 in range(2):
        wh, wl = weights(w_ref, row, 8 + p0, LOST, 0, count)
        spread.append(jnp.concatenate([wh, wh, wl], axis=1))
    group = lax.broadcasted_iota(jnp.int32, (8, HALF), 1) // WIDTH
    sends = []
    for g, rows in enumerate(groups):
        loads[g][0].wait()
        for half in range(2):
            lanes = slice(half * HALF, (half + 1) * HALF)
            x = [back[half * 16 + c, rows, :] for c in range(16)]
            for bit in (1, 2, 4, 8):
                upper = (group // bit) % 2 == 1
                for c in range(16):
                    if not c & bit:
                        low, high = x[c], x[c + bit]
                        x[c] = jnp.where(upper, pltpu.roll(high, bit * WIDTH, 1), low)
                        x[c + bit] = jnp.where(upper, high, pltpu.roll(low, HALF - bit * WIDTH, 1))
            if half == 0:
                for load in loads[g][1:]:
                    load.wait()
            for p0 in range(2):
                sh, sl = halves(jnp.concatenate(x[p0 * LOST : (p0 + 1) * LOST], axis=0))
                stacked = jnp.concatenate([sh, sl, sh], axis=0)
                total = lax.dot_general(spread[p0], stacked, NN, preferred_element_type=F32)
                total = total.reshape(OCC, 8, HALF)
                out[p0, :, rows, lanes] = u[p0, :, rows, lanes] + total * r[p0, :, rows, lanes]
        sends.append(pltpu.make_async_copy(out.at[:, :, rows], o_ref.at[:, :, rows], outs.at[g]))
        sends[-1].start()
    for send in sends:
        send.wait()


def finish(row, back, w, u, r):
    return pl.pallas_call(
        finish_kernel,
        out_shape=jax.ShapeDtypeStruct(u.shape, F32),
        in_specs=[SMEM, HBM, VMEM, HBM, HBM],
        out_specs=HBM,
        scratch_shapes=[pltpu.VMEM(back.shape, F32)]
        + [pltpu.VMEM(u.shape, F32)] * 3
        + [pltpu.SemaphoreType.DMA((3, WIDTH // 8)), pltpu.SemaphoreType.DMA((WIDTH // 8,))],
        compiler_params=pltpu.CompilerParams(vmem_limit_bytes=62_500_000),
        name="finish",
    )(row, back, w, u, r)


def on_device(amplitudes, first_rotation, second_rotation, pair_weights, denominators):
    row = lax.axis_index("occi")
    column = lax.axis_index("occj")
    p = 2 * row + column // OCC
    ahead = jnp.mod(column % OCC - p, OCC)
    wins = ((ahead >= 1) & (ahead <= 7)) | ((ahead == 8) & (p < 8))
    mode = jnp.where(ahead == 0, 2, jnp.where(wins, 0, 1)).astype(jnp.int32).reshape(1)
    row_here = row.astype(jnp.int32).reshape(1)

    z = transform(mode, amplitudes[0], first_rotation, second_rotation)
    z = lax.all_to_all(z.reshape(COLS, WIDTH, VIRT), "occj", split_axis=0, concat_axis=0, tiled=True)
    z = z.reshape(2, ROWS, 2, WIDTH, VIRT)

    def exchange(step):
        out = lax.dynamic_index_in_dim(z, jnp.mod(row + step, ROWS), 1, keepdims=False)
        return lax.ppermute(out, "occi", [(r, (r + step) % ROWS) for r in range(ROWS)])

    got = {ROWS - step: exchange(step) for step in range(1, ROWS)}
    lost = lost_items(row_here, z, got[7], got[6], got[5], got[4])
    back = lax.all_to_all(lost.reshape(COLS, WIDTH, HALF), "occj", split_axis=0, concat_axis=0, tiled=True)
    u, r = kept_items(row_here, z, got[4], got[3], got[2], got[1], pair_weights, denominators)
    return finish(row_here, back, pair_weights, u, r)


def solution(mesh):
    placed = (P(("occi", "occj"), None, None), P(), P(), P(), P("occi", None, "occj", None))
    return jax.shard_map(
        on_device,
        mesh=mesh,
        in_specs=placed,
        out_specs=P("occi", None, "occj", None),
        check_vma=False,
    )
```

```python
import jax
import jax.numpy as jnp
from jax import lax
from jax.experimental import pallas as pl
from jax.experimental.pallas import tpu as pltpu
from jax.sharding import PartitionSpec as P

OCC = 16
VIRT = 768
ROWS = 8
COLS = 32
WIDTH = VIRT // COLS
HALF = VIRT // 2
CHUNK = 256
PARTS = VIRT // CHUNK
KEPT = 9
LOST = 8
F32 = jnp.float32
BF16 = jnp.bfloat16
NT = (((1,), (1,)), ((), ()))
NN = (((1,), (0,)), ((), ()))
HBM = pl.BlockSpec(memory_space=pltpu.HBM)
VMEM = pl.BlockSpec(memory_space=pltpu.VMEM)
SMEM = pl.BlockSpec(memory_space=pltpu.SMEM)


def halves(x):
    high = x.astype(BF16)
    return high, (x - high.astype(F32)).astype(BF16)


def dot3(lh, ll, rh, rl, dims):
    def one(a, b):
        return lax.dot_general(a, b, dims, preferred_element_type=F32)

    return one(lh, rh) + (one(lh, rl) + one(ll, rh))


def transform_kernel(mode_ref, t_ref, a_ref, b_ref, z_ref, t, a, b, z, t3, a3, pair, ins, outs):
    mode = mode_ref[0]
    mine = jnp.where(mode == 0, 1, 0)
    chunks = [slice(i * CHUNK, (i + 1) * CHUNK) for i in range(PARTS)]
    thirds = [slice(i * VIRT, (i + 1) * VIRT) for i in range(3)]
    loads = []
    for n, (src, dst) in enumerate(((t_ref, t), (a_ref, a), (b_ref, b))):
        loads.append([pltpu.make_async_copy(src.at[r], dst.at[r], ins.at[n, i]) for i, r in enumerate(chunks)])
    for load in loads[0] + loads[1]:
        load.start()

    def put(slot, rows, x, right):
        h, l = halves(x)
        pair[slot, rows, thirds[0]] = h
        pair[slot, rows, thirds[1]] = jnp.where(right, l, h)
        pair[slot, rows, thirds[2]] = jnp.where(right, h, l)

    for i, (load, r) in enumerate(zip(loads[0], chunks)):
        load.wait()
        h, l = halves(t[r, :])
        for n, x in enumerate((h, l, h)):
            t3[n * VIRT + i * CHUNK : n * VIRT + (i + 1) * CHUNK, :] = x
    for load in loads[2]:
        load.start()
    for load, r in zip(loads[1], chunks):
        load.wait()
        h, l = halves(a[r, :])
        for third, x in zip(thirds, (h, h, l)):
            a3[r, third] = x
        put(mine, r, lax.dot_general(a3[r, :], t3[...], NN, preferred_element_type=F32), mode == 0)
    for load, r in zip(loads[2], chunks):
        load.wait()
        put(1 - mine, r, b[r, :], mode != 0)
    sends = [pltpu.make_async_copy(z.at[r], z_ref.at[r], outs.at[i]) for i, r in enumerate(chunks)]
    for send, r in zip(sends, chunks):
        z[r, :] = lax.dot_general(pair[0, r, :], pair[1], NT, preferred_element_type=F32)

        @pl.when(mode != 2)
        def _():
            send.start()

    @pl.when(mode == 2)
    def _():
        tiles = [slice(i * 128, (i + 1) * 128) for i in range(VIRT // 128)]
        for n, i in enumerate(tiles):
            for j in tiles[n:]:
                mean = 0.5 * (z[i, j] + z[j, i].T)
                z[i, j] = mean
                if i != j:
                    z[j, i] = mean.T
        for send in sends:
            send.start()

    for send in sends:
        send.wait()


def transform(mode, t, a, b):
    return pl.pallas_call(
        transform_kernel,
        out_shape=jax.ShapeDtypeStruct((VIRT, VIRT), F32),
        in_specs=[SMEM, HBM, HBM, HBM],
        out_specs=HBM,
        scratch_shapes=[pltpu.VMEM((VIRT, VIRT), F32)] * 4
        + [pltpu.VMEM((3 * VIRT, VIRT), BF16), pltpu.VMEM((VIRT, 3 * VIRT), BF16), pltpu.VMEM((2, VIRT, 3 * VIRT), BF16)]
        + [pltpu.SemaphoreType.DMA((3, PARTS)), pltpu.SemaphoreType.DMA((PARTS,))],
        compiler_params=pltpu.CompilerParams(vmem_limit_bytes=63_500_000),
        name="transform",
    )(mode, t, a, b)


STEPS = (7, 6, 5, 4, 0)


def lost_kernel(row_ref, z_hbm, g7, g6, g5, g4, o_ref, own, other, stage, turned, ins, outs):
    row = row_ref[0]
    loads = []
    for i, (step, got) in enumerate(zip(STEPS, (g7, g6, g5, g4))):
        there = lax.rem(row + step, ROWS)
        loads.append(
            [pltpu.make_async_copy(z_hbm.at[p0, there], own.at[p0, i], ins.at[i, p0]) for p0 in range(2)]
            + [pltpu.make_async_copy(got, other.at[i], ins.at[i, 2])]
        )
    loads.append([pltpu.make_async_copy(z_hbm.at[p0, row, 1 - p0], own.at[p0, 4, 1 - p0], ins.at[4, p0]) for p0 in range(2)])
    for group in loads:
        for load in group:
            load.start()
    for i, group in enumerate(loads):
        for load in group:
            load.wait()
        for p0 in range(2):
            for m in range(LOST):
                partner = 8 + p0 + m
                if (partner // 2) % ROWS == STEPS[i]:
                    q0 = partner % 2
                    second = own[1 - p0, i, p0] if i == 4 else other[i, q0, p0]
                    at = (p0 * LOST + m) * WIDTH
                    stage[at : at + WIDTH, :] = own[p0, i, q0] + second
    sends = []
    for i in range(PARTS):
        rows = slice(i * CHUNK, (i + 1) * CHUNK)
        turned[rows, :] = stage[:, rows].T
        sends.append(pltpu.make_async_copy(turned.at[rows], o_ref.at[rows], outs.at[i]))
        sends[-1].start()
    for send in sends:
        send.wait()


def lost_items(row, z, *got):
    return pl.pallas_call(
        lost_kernel,
        out_shape=jax.ShapeDtypeStruct((VIRT, HALF), F32),
        in_specs=[SMEM] + [HBM] * 5,
        out_specs=HBM,
        scratch_shapes=[
            pltpu.VMEM((2, 5, 2, WIDTH, VIRT), F32),
            pltpu.VMEM((4, 2, 2, WIDTH, VIRT), F32),
            pltpu.VMEM((HALF, VIRT), F32),
            pltpu.VMEM((VIRT, HALF), F32),
            pltpu.SemaphoreType.DMA((5, 3)),
            pltpu.SemaphoreType.DMA((PARTS,)),
        ],
        compiler_params=pltpu.CompilerParams(vmem_limit_bytes=63_500_000),
        name="lost_items",
    )(row, z, *got)


def weights(w_ref, row, first, many, tie, count):
    def iota(shape, dim):
        return lax.broadcasted_iota(jnp.int32, shape, dim)

    out = OCC * 8
    pick = (iota((out, OCC), 0) // 8 == iota((out, OCC), 1)).astype(F32)
    m = iota((OCC, many * 8), 1) // 8
    index = (m + (first + 2 * row)) % OCC
    chosen = jnp.where(iota((OCC, many * 8), 0) == index, jnp.where(m == tie, count, 1.0), 0.0)
    full = lax.dot_general(pick, w_ref[...], NT, precision=lax.Precision.HIGHEST, preferred_element_type=F32)
    full = lax.dot_general(full, chosen, NN, precision=lax.Precision.HIGHEST, preferred_element_type=F32)
    same = iota((out, many * 8), 0) % 8 == iota((out, many * 8), 1) % 8
    return halves(jnp.where(same, full, 0.0))


def kept_kernel(row_ref, z_ref, g4, g3, g2, g1, w_ref, d_ref, u_ref, r_ref):
    row = row_ref[0]
    got = {4: g4, 3: g3, 2: g2, 1: g1}
    count = jnp.where(row < ROWS // 2, 1.0, 0.0)
    for p0 in range(2):
        wh, wl = weights(w_ref, row, p0, KEPT, KEPT - 1, count)
        for g in range(WIDTH // 8):
            rows = slice(g * 8, (g + 1) * 8)
            parts = []
            for n in range(p0, p0 + KEPT):
                there, q0 = n // 2, n % 2
                first = z_ref[p0, lax.rem(row + there, ROWS), q0, rows, :]
                second = got[there][q0, p0, rows, :] if there else z_ref[q0, row, p0, rows, :]
                parts.append(first + second)
            sh, sl = halves(jnp.concatenate(parts, axis=0))
            total = dot3(wh, wl, sh, sl, NN).reshape(OCC, 8, VIRT)
            scale = 1.0 / d_ref[p0, :, rows, :]
            r_ref[p0, :, rows, :] = scale
            u_ref[p0, :, rows, :] = total * scale


def kept_items(row, z, *rest):
    shape = jax.ShapeDtypeStruct(rest[-1].shape, F32)
    return pl.pallas_call(
        kept_kernel,
        out_shape=(shape, shape),
        in_specs=[SMEM] + [VMEM] * 7,
        out_specs=(VMEM, VMEM),
        compiler_params=pltpu.CompilerParams(vmem_limit_bytes=40 * 2**20),
        cost_estimate=pl.CostEstimate(flops=10**11, bytes_accessed=12 * 10**6, transcendentals=0),
        name="kept_items",
    )(row, z, *rest)


def finish_kernel(row_ref, back_hbm, w_ref, u_hbm, r_hbm, o_ref, back, u, r, out, ins, outs):
    row = row_ref[0]
    groups = [slice(g * 8, (g + 1) * 8) for g in range(WIDTH // 8)]
    loads = []
    for g, rows in enumerate(groups):
        loads.append(
            [
                pltpu.make_async_copy(back_hbm.at[:, rows], back.at[:, rows], ins.at[0, g]),
                pltpu.make_async_copy(u_hbm.at[:, :, rows], u.at[:, :, rows], ins.at[1, g]),
                pltpu.make_async_copy(r_hbm.at[:, :, rows], r.at[:, :, rows], ins.at[2, g]),
            ]
        )
        for load in loads[-1]:
            load.start()
    count = jnp.where(row < ROWS // 2, 0.0, 1.0)
    spread = []
    for p0 in range(2):
        wh, wl = weights(w_ref, row, 8 + p0, LOST, 0, count)
        spread.append(jnp.concatenate([wh, wh, wl], axis=1))
    group = lax.broadcasted_iota(jnp.int32, (8, HALF), 1) // WIDTH
    sends = []
    for g, rows in enumerate(groups):
        loads[g][0].wait()
        for half in range(2):
            lanes = slice(half * HALF, (half + 1) * HALF)
            x = [back[half * 16 + c, rows, :] for c in range(16)]
            for bit in (1, 2, 4, 8):
                upper = (group // bit) % 2 == 1
                for c in range(16):
                    if not c & bit:
                        low, high = x[c], x[c + bit]
                        x[c] = jnp.where(upper, pltpu.roll(high, bit * WIDTH, 1), low)
                        x[c + bit] = jnp.where(upper, high, pltpu.roll(low, HALF - bit * WIDTH, 1))
            if half == 0:
                for load in loads[g][1:]:
                    load.wait()
            for p0 in range(2):
                sh, sl = halves(jnp.concatenate(x[p0 * LOST : (p0 + 1) * LOST], axis=0))
                stacked = jnp.concatenate([sh, sl, sh], axis=0)
                total = lax.dot_general(spread[p0], stacked, NN, preferred_element_type=F32)
                total = total.reshape(OCC, 8, HALF)
                out[p0, :, rows, lanes] = u[p0, :, rows, lanes] + total * r[p0, :, rows, lanes]
        sends.append(pltpu.make_async_copy(out.at[:, :, rows], o_ref.at[:, :, rows], outs.at[g]))
        sends[-1].start()
    for send in sends:
        send.wait()


def finish(row, back, w, u, r):
    return pl.pallas_call(
        finish_kernel,
        out_shape=jax.ShapeDtypeStruct(u.shape, F32),
        in_specs=[SMEM, HBM, VMEM, HBM, HBM],
        out_specs=HBM,
        scratch_shapes=[pltpu.VMEM(back.shape, F32)]
        + [pltpu.VMEM(u.shape, F32)] * 3
        + [pltpu.SemaphoreType.DMA((3, WIDTH // 8)), pltpu.SemaphoreType.DMA((WIDTH // 8,))],
        compiler_params=pltpu.CompilerParams(vmem_limit_bytes=62_500_000),
        name="finish",
    )(row, back, w, u, r)


def on_device(amplitudes, first_rotation, second_rotation, pair_weights, denominators):
    row = lax.axis_index("occi")
    column = lax.axis_index("occj")
    p = 2 * row + column // OCC
    ahead = jnp.mod(column % OCC - p, OCC)
    wins = ((ahead >= 1) & (ahead <= 7)) | ((ahead == 8) & (p < 8))
    mode = jnp.where(ahead == 0, 2, jnp.where(wins, 0, 1)).astype(jnp.int32).reshape(1)
    row_here = row.astype(jnp.int32).reshape(1)

    z = transform(mode, amplitudes[0], first_rotation, second_rotation)
    z = lax.all_to_all(z.reshape(COLS, WIDTH, VIRT), "occj", split_axis=0, concat_axis=0, tiled=True)
    z = z.reshape(2, ROWS, 2, WIDTH, VIRT)

    def leaving(step):
        return lax.dynamic_index_in_dim(z, jnp.mod(row + step, ROWS), 1, keepdims=False)

    def arriving(step, out):
        return lax.ppermute(out, "occi", [(r, (r + step) % ROWS) for r in range(ROWS)])

    got = {ROWS - step: arriving(step, leaving(step)) for step in (1, 2, 3, 4)}
    first, rest = lax.optimization_barrier(
        ([got[n] for n in (7, 6, 5, 4)], [leaving(step) for step in (5, 6, 7)])
    )
    got.update(zip((7, 6, 5, 4), first))
    got.update({ROWS - step: arriving(step, out) for step, out in zip((5, 6, 7), rest)})
    lost = lost_items(row_here, z, got[7], got[6], got[5], got[4])
    back = lax.all_to_all(lost.reshape(COLS, WIDTH, HALF), "occj", split_axis=0, concat_axis=0, tiled=True)
    u, r = kept_items(row_here, z, got[4], got[3], got[2], got[1], pair_weights, denominators)
    return finish(row_here, back, pair_weights, u, r)


def solution(mesh):
    placed = (P(("occi", "occj"), None, None), P(), P(), P(), P("occi", None, "occj", None))
    return jax.shard_map(
        on_device,
        mesh=mesh,
        in_specs=placed,
        out_specs=P("occi", None, "occj", None),
        check_vma=False,
    )
```

```python
import jax
import jax.numpy as jnp
from jax import lax
from jax.experimental import pallas as pl
from jax.experimental.pallas import tpu as pltpu
from jax.sharding import PartitionSpec as P

OCC = 16
VIRT = 768
ROWS = 8
COLS = 32
WIDTH = VIRT // COLS
HALF = VIRT // 2
CHUNK = 256
PARTS = VIRT // CHUNK
KEPT = 9
LOST = 8
F32 = jnp.float32
BF16 = jnp.bfloat16
NT = (((1,), (1,)), ((), ()))
NN = (((1,), (0,)), ((), ()))
HBM = pl.BlockSpec(memory_space=pltpu.HBM)
VMEM = pl.BlockSpec(memory_space=pltpu.VMEM)
SMEM = pl.BlockSpec(memory_space=pltpu.SMEM)


def halves(x):
    high = x.astype(BF16)
    return high, (x - high.astype(F32)).astype(BF16)


def dot3(lh, ll, rh, rl, dims):
    def one(a, b):
        return lax.dot_general(a, b, dims, preferred_element_type=F32)

    return one(lh, rh) + (one(lh, rl) + one(ll, rh))


def transform_kernel(mode_ref, t_ref, a_ref, b_ref, z_ref, t, a, b, z, t3, a3, pair, ins, outs):
    mode = mode_ref[0]
    mine = jnp.where(mode == 0, 1, 0)
    chunks = [slice(i * CHUNK, (i + 1) * CHUNK) for i in range(PARTS)]
    thirds = [slice(i * VIRT, (i + 1) * VIRT) for i in range(3)]
    loads = []
    for n, (src, dst) in enumerate(((t_ref, t), (a_ref, a), (b_ref, b))):
        loads.append([pltpu.make_async_copy(src.at[r], dst.at[r], ins.at[n, i]) for i, r in enumerate(chunks)])
    for load in loads[0] + loads[1]:
        load.start()

    def put(slot, rows, x, right):
        h, l = halves(x)
        pair[slot, rows, thirds[0]] = h
        pair[slot, rows, thirds[1]] = jnp.where(right, l, h)
        pair[slot, rows, thirds[2]] = jnp.where(right, h, l)

    for i, (load, r) in enumerate(zip(loads[0], chunks)):
        load.wait()
        h, l = halves(t[r, :])
        for n, x in enumerate((h, l, h)):
            t3[n * VIRT + i * CHUNK : n * VIRT + (i + 1) * CHUNK, :] = x
    for load in loads[2]:
        load.start()
    for load, r in zip(loads[1], chunks):
        load.wait()
        h, l = halves(a[r, :])
        for third, x in zip(thirds, (h, h, l)):
            a3[r, third] = x
        put(mine, r, lax.dot_general(a3[r, :], t3[...], NN, preferred_element_type=F32), mode == 0)
    for load, r in zip(loads[2], chunks):
        load.wait()
        put(1 - mine, r, b[r, :], mode != 0)
    sends = [pltpu.make_async_copy(z.at[r], z_ref.at[r], outs.at[i]) for i, r in enumerate(chunks)]
    for send, r in zip(sends, chunks):
        z[r, :] = lax.dot_general(pair[0, r, :], pair[1], NT, preferred_element_type=F32)

        @pl.when(mode != 2)
        def _():
            send.start()

    @pl.when(mode == 2)
    def _():
        tiles = [slice(i * 128, (i + 1) * 128) for i in range(VIRT // 128)]
        for n, i in enumerate(tiles):
            for j in tiles[n:]:
                mean = 0.5 * (z[i, j] + z[j, i].T)
                z[i, j] = mean
                if i != j:
                    z[j, i] = mean.T
        for send in sends:
            send.start()

    for send in sends:
        send.wait()


def transform(mode, t, a, b):
    return pl.pallas_call(
        transform_kernel,
        out_shape=jax.ShapeDtypeStruct((VIRT, VIRT), F32),
        in_specs=[SMEM, HBM, HBM, HBM],
        out_specs=HBM,
        scratch_shapes=[pltpu.VMEM((VIRT, VIRT), F32)] * 4
        + [pltpu.VMEM((3 * VIRT, VIRT), BF16), pltpu.VMEM((VIRT, 3 * VIRT), BF16), pltpu.VMEM((2, VIRT, 3 * VIRT), BF16)]
        + [pltpu.SemaphoreType.DMA((3, PARTS)), pltpu.SemaphoreType.DMA((PARTS,))],
        compiler_params=pltpu.CompilerParams(vmem_limit_bytes=63_500_000),
        name="transform",
    )(mode, t, a, b)


def lost_kernel(row_ref, z_ref, e_ref, o_ref, stage, turned, outs):
    row = row_ref[0]
    for p0 in range(2):
        for m in range(LOST):
            partner = 8 + p0 + m
            there, q0 = lax.rem(row + (partner // 2) % ROWS, ROWS), partner % 2
            at = (p0 * LOST + m) * WIDTH
            stage[at : at + WIDTH, :] = z_ref[p0, there, q0] + e_ref[there, q0, p0]
    sends = []
    for i in range(PARTS):
        rows = slice(i * CHUNK, (i + 1) * CHUNK)
        turned[rows, :] = stage[:, rows].T
        sends.append(pltpu.make_async_copy(turned.at[rows], o_ref.at[rows], outs.at[i]))
        sends[-1].start()
    for send in sends:
        send.wait()


def lost_items(row, z, e):
    return pl.pallas_call(
        lost_kernel,
        out_shape=jax.ShapeDtypeStruct((VIRT, HALF), F32),
        in_specs=[SMEM, VMEM, VMEM],
        out_specs=HBM,
        scratch_shapes=[
            pltpu.VMEM((HALF, VIRT), F32),
            pltpu.VMEM((VIRT, HALF), F32),
            pltpu.SemaphoreType.DMA((PARTS,)),
        ],
        compiler_params=pltpu.CompilerParams(vmem_limit_bytes=40_000_000),
        name="lost_items",
    )(row, z, e)


def weights(w_ref, row, first, many, tie, count):
    def iota(shape, dim):
        return lax.broadcasted_iota(jnp.int32, shape, dim)

    out = OCC * 8
    pick = (iota((out, OCC), 0) // 8 == iota((out, OCC), 1)).astype(F32)
    m = iota((OCC, many * 8), 1) // 8
    index = (m + (first + 2 * row)) % OCC
    chosen = jnp.where(iota((OCC, many * 8), 0) == index, jnp.where(m == tie, count, 1.0), 0.0)
    full = lax.dot_general(pick, w_ref[...], NT, precision=lax.Precision.HIGHEST, preferred_element_type=F32)
    full = lax.dot_general(full, chosen, NN, precision=lax.Precision.HIGHEST, preferred_element_type=F32)
    same = iota((out, many * 8), 0) % 8 == iota((out, many * 8), 1) % 8
    return halves(jnp.where(same, full, 0.0))


def kept_kernel(row_ref, z_ref, e_ref, w_ref, d_ref, u_ref, r_ref):
    row = row_ref[0]
    count = jnp.where(row < ROWS // 2, 1.0, 0.0)
    for p0 in range(2):
        wh, wl = weights(w_ref, row, p0, KEPT, KEPT - 1, count)
        for g in range(WIDTH // 8):
            rows = slice(g * 8, (g + 1) * 8)
            there = [lax.rem(row + n // 2, ROWS) for n in range(p0, p0 + KEPT)]
            parts = [
                z_ref[p0, t, n % 2, rows, :] + e_ref[t, n % 2, p0, rows, :]
                for t, n in zip(there, range(p0, p0 + KEPT))
            ]
            sh, sl = halves(jnp.concatenate(parts, axis=0))
            total = dot3(wh, wl, sh, sl, NN).reshape(OCC, 8, VIRT)
            scale = 1.0 / d_ref[p0, :, rows, :]
            r_ref[p0, :, rows, :] = scale
            u_ref[p0, :, rows, :] = total * scale


def kept_items(row, z, e, w, d):
    shape = jax.ShapeDtypeStruct(d.shape, F32)
    return pl.pallas_call(
        kept_kernel,
        out_shape=(shape, shape),
        in_specs=[SMEM] + [VMEM] * 4,
        out_specs=(VMEM, VMEM),
        compiler_params=pltpu.CompilerParams(vmem_limit_bytes=40 * 2**20),
        cost_estimate=pl.CostEstimate(flops=2 * 10**9, bytes_accessed=12 * 10**6, transcendentals=0),
        name="kept_items",
    )(row, z, e, w, d)


def finish_kernel(row_ref, back, w_ref, u_hbm, r_hbm, o_ref, u, r, out, ins, outs):
    row = row_ref[0]
    groups = [slice(g * 8, (g + 1) * 8) for g in range(WIDTH // 8)]
    loads = []
    for g, rows in enumerate(groups):
        loads.append(
            [
                pltpu.make_async_copy(u_hbm.at[:, :, rows], u.at[:, :, rows], ins.at[0, g]),
                pltpu.make_async_copy(r_hbm.at[:, :, rows], r.at[:, :, rows], ins.at[1, g]),
            ]
        )
        for load in loads[-1]:
            load.start()
    count = jnp.where(row < ROWS // 2, 0.0, 1.0)
    spread = []
    for p0 in range(2):
        wh, wl = weights(w_ref, row, 8 + p0, LOST, 0, count)
        spread.append(jnp.concatenate([wh, wh, wl], axis=1))
    group = lax.broadcasted_iota(jnp.int32, (8, HALF), 1) // WIDTH
    sends = []
    for g, rows in enumerate(groups):
        for half in range(2):
            lanes = slice(half * HALF, (half + 1) * HALF)
            x = [back[half * 16 + c, rows, :] for c in range(16)]
            for bit in (1, 2, 4, 8):
                upper = (group // bit) % 2 == 1
                for c in range(16):
                    if not c & bit:
                        low, high = x[c], x[c + bit]
                        x[c] = jnp.where(upper, pltpu.roll(high, bit * WIDTH, 1), low)
                        x[c + bit] = jnp.where(upper, high, pltpu.roll(low, HALF - bit * WIDTH, 1))
            if half == 0:
                for load in loads[g]:
                    load.wait()
            for p0 in range(2):
                sh, sl = halves(jnp.concatenate(x[p0 * LOST : (p0 + 1) * LOST], axis=0))
                stacked = jnp.concatenate([sh, sl, sh], axis=0)
                total = lax.dot_general(spread[p0], stacked, NN, preferred_element_type=F32)
                total = total.reshape(OCC, 8, HALF)
                out[p0, :, rows, lanes] = u[p0, :, rows, lanes] + total * r[p0, :, rows, lanes]
        sends.append(pltpu.make_async_copy(out.at[:, :, rows], o_ref.at[:, :, rows], outs.at[g]))
        sends[-1].start()
    for send in sends:
        send.wait()


def finish(row, back, w, u, r):
    return pl.pallas_call(
        finish_kernel,
        out_shape=jax.ShapeDtypeStruct(u.shape, F32),
        in_specs=[SMEM, VMEM, VMEM, HBM, HBM],
        out_specs=HBM,
        scratch_shapes=[pltpu.VMEM(u.shape, F32)] * 3
        + [pltpu.SemaphoreType.DMA((2, WIDTH // 8)), pltpu.SemaphoreType.DMA((WIDTH // 8,))],
        compiler_params=pltpu.CompilerParams(vmem_limit_bytes=54_000_000),
        name="finish",
    )(row, back, w, u, r)


def on_device(amplitudes, first_rotation, second_rotation, pair_weights, denominators):
    row = lax.axis_index("occi")
    column = lax.axis_index("occj")
    p = 2 * row + column // OCC
    ahead = jnp.mod(column % OCC - p, OCC)
    wins = ((ahead >= 1) & (ahead <= 7)) | ((ahead == 8) & (p < 8))
    mode = jnp.where(ahead == 0, 2, jnp.where(wins, 0, 1)).astype(jnp.int32).reshape(1)
    row_here = row.astype(jnp.int32).reshape(1)

    z = transform(mode, amplitudes[0], first_rotation, second_rotation)
    z = lax.all_to_all(z.reshape(COLS, WIDTH, VIRT), "occj", split_axis=0, concat_axis=0, tiled=True)
    z = z.reshape(2, ROWS, 2, WIDTH, VIRT)
    e = lax.all_to_all(jnp.swapaxes(z, 0, 1), "occi", split_axis=0, concat_axis=0, tiled=True)
    lost = lost_items(row_here, z, e)
    back = lax.all_to_all(lost.reshape(COLS, WIDTH, HALF), "occj", split_axis=0, concat_axis=0, tiled=True)
    u, r = kept_items(row_here, z, e, pair_weights, denominators)
    return finish(row_here, back, pair_weights, u, r)


def solution(mesh):
    placed = (P(("occi", "occj"), None, None), P(), P(), P(), P("occi", None, "occj", None))
    return jax.shard_map(
        on_device,
        mesh=mesh,
        in_specs=placed,
        out_specs=P("occi", None, "occj", None),
        check_vma=False,
    )
```

```python
import jax
import jax.numpy as jnp
from jax import lax
from jax.experimental import pallas as pl
from jax.experimental.pallas import tpu as pltpu
from jax.sharding import PartitionSpec as P

OCC = 16
VIRT = 768
ROWS = 8
COLS = 32
WIDTH = VIRT // COLS
HALF = VIRT // 2
CHUNK = 256
PARTS = VIRT // CHUNK
KEPT = 9
LOST = 8
F32 = jnp.float32
BF16 = jnp.bfloat16
NT = (((1,), (1,)), ((), ()))
NN = (((1,), (0,)), ((), ()))
HBM = pl.BlockSpec(memory_space=pltpu.HBM)
VMEM = pl.BlockSpec(memory_space=pltpu.VMEM)
SMEM = pl.BlockSpec(memory_space=pltpu.SMEM)


def halves(x):
    high = x.astype(BF16)
    return high, (x - high.astype(F32)).astype(BF16)


def dot3(lh, ll, rh, rl, dims):
    def one(a, b):
        return lax.dot_general(a, b, dims, preferred_element_type=F32)

    return one(lh, rh) + (one(lh, rl) + one(ll, rh))


def transform_kernel(mode_ref, t_ref, a_ref, b_ref, z, t, a, b, t3, a3, pair, ins):
    mode = mode_ref[0]
    mine = jnp.where(mode == 0, 1, 0)
    chunks = [slice(i * CHUNK, (i + 1) * CHUNK) for i in range(PARTS)]
    thirds = [slice(i * VIRT, (i + 1) * VIRT) for i in range(3)]
    loads = []
    for n, (src, dst) in enumerate(((t_ref, t), (a_ref, a), (b_ref, b))):
        loads.append([pltpu.make_async_copy(src.at[r], dst.at[r], ins.at[n, i]) for i, r in enumerate(chunks)])
    for load in loads[0] + loads[1]:
        load.start()

    def put(slot, rows, x, right):
        h, l = halves(x)
        pair[slot, rows, thirds[0]] = h
        pair[slot, rows, thirds[1]] = jnp.where(right, l, h)
        pair[slot, rows, thirds[2]] = jnp.where(right, h, l)

    for i, (load, r) in enumerate(zip(loads[0], chunks)):
        load.wait()
        h, l = halves(t[r, :])
        for n, x in enumerate((h, l, h)):
            t3[n * VIRT + i * CHUNK : n * VIRT + (i + 1) * CHUNK, :] = x
    for load in loads[2]:
        load.start()
    for load, r in zip(loads[1], chunks):
        load.wait()
        h, l = halves(a[r, :])
        for third, x in zip(thirds, (h, h, l)):
            a3[r, third] = x
        put(mine, r, lax.dot_general(a3[r, :], t3[...], NN, preferred_element_type=F32), mode == 0)
    for load, r in zip(loads[2], chunks):
        load.wait()
        put(1 - mine, r, b[r, :], mode != 0)
    for r in chunks:
        z[r, :] = lax.dot_general(pair[0, r, :], pair[1], NT, preferred_element_type=F32)

    @pl.when(mode == 2)
    def _():
        tiles = [slice(i * 128, (i + 1) * 128) for i in range(VIRT // 128)]
        for n, i in enumerate(tiles):
            for j in tiles[n:]:
                mean = 0.5 * (z[i, j] + z[j, i].T)
                z[i, j] = mean
                if i != j:
                    z[j, i] = mean.T


def transform(mode, t, a, b):
    return pl.pallas_call(
        transform_kernel,
        out_shape=jax.ShapeDtypeStruct((VIRT, VIRT), F32),
        in_specs=[SMEM, HBM, HBM, HBM],
        out_specs=VMEM,
        scratch_shapes=[pltpu.VMEM((VIRT, VIRT), F32)] * 3
        + [pltpu.VMEM((3 * VIRT, VIRT), BF16), pltpu.VMEM((VIRT, 3 * VIRT), BF16), pltpu.VMEM((2, VIRT, 3 * VIRT), BF16)]
        + [pltpu.SemaphoreType.DMA((3, PARTS))],
        compiler_params=pltpu.CompilerParams(vmem_limit_bytes=54_000_000),
        name="transform",
    )(mode, t, a, b)


def lost_kernel(row_ref, z_ref, e_ref, o_ref, stage):
    row = row_ref[0]
    for p0 in range(2):
        for m in range(LOST):
            partner = 8 + p0 + m
            there, q0 = lax.rem(row + (partner // 2) % ROWS, ROWS), partner % 2
            at = (p0 * LOST + m) * WIDTH
            stage[at : at + WIDTH, :] = z_ref[p0, there, q0] + e_ref[there, q0, p0]
    for i in range(PARTS):
        rows = slice(i * CHUNK, (i + 1) * CHUNK)
        o_ref[rows, :] = stage[:, rows].T


def lost_items(row, z, e):
    return pl.pallas_call(
        lost_kernel,
        out_shape=jax.ShapeDtypeStruct((VIRT, HALF), F32),
        in_specs=[SMEM, VMEM, VMEM],
        out_specs=VMEM,
        scratch_shapes=[pltpu.VMEM((HALF, VIRT), F32)],
        compiler_params=pltpu.CompilerParams(vmem_limit_bytes=48_000_000),
        name="lost_items",
    )(row, z, e)


def weights(w_ref, row, first, many, tie, count):
    def iota(shape, dim):
        return lax.broadcasted_iota(jnp.int32, shape, dim)

    out = OCC * 8
    pick = (iota((out, OCC), 0) // 8 == iota((out, OCC), 1)).astype(F32)
    m = iota((OCC, many * 8), 1) // 8
    index = (m + (first + 2 * row)) % OCC
    chosen = jnp.where(iota((OCC, many * 8), 0) == index, jnp.where(m == tie, count, 1.0), 0.0)
    full = lax.dot_general(pick, w_ref[...], NT, precision=lax.Precision.HIGHEST, preferred_element_type=F32)
    full = lax.dot_general(full, chosen, NN, precision=lax.Precision.HIGHEST, preferred_element_type=F32)
    same = iota((out, many * 8), 0) % 8 == iota((out, many * 8), 1) % 8
    return halves(jnp.where(same, full, 0.0))


def kept_kernel(row_ref, z_ref, e_ref, w_ref, d_ref, u_ref, r_ref):
    row = row_ref[0]
    count = jnp.where(row < ROWS // 2, 1.0, 0.0)
    for p0 in range(2):
        wh, wl = weights(w_ref, row, p0, KEPT, KEPT - 1, count)
        for g in range(WIDTH // 8):
            rows = slice(g * 8, (g + 1) * 8)
            there = [lax.rem(row + n // 2, ROWS) for n in range(p0, p0 + KEPT)]
            parts = [
                z_ref[p0, t, n % 2, rows, :] + e_ref[t, n % 2, p0, rows, :]
                for t, n in zip(there, range(p0, p0 + KEPT))
            ]
            sh, sl = halves(jnp.concatenate(parts, axis=0))
            total = dot3(wh, wl, sh, sl, NN).reshape(OCC, 8, VIRT)
            scale = 1.0 / d_ref[p0, :, rows, :]
            r_ref[p0, :, rows, :] = scale
            u_ref[p0, :, rows, :] = total * scale


def kept_items(row, z, e, w, d):
    shape = jax.ShapeDtypeStruct(d.shape, F32)
    return pl.pallas_call(
        kept_kernel,
        out_shape=(shape, shape),
        in_specs=[SMEM] + [VMEM] * 4,
        out_specs=(VMEM, VMEM),
        compiler_params=pltpu.CompilerParams(vmem_limit_bytes=40 * 2**20),
        cost_estimate=pl.CostEstimate(flops=2 * 10**9, bytes_accessed=12 * 10**6, transcendentals=0),
        name="kept_items",
    )(row, z, e, w, d)


def finish_kernel(row_ref, back, w_ref, u_hbm, r_hbm, o_ref, u, r, out, ins, outs):
    row = row_ref[0]
    groups = [slice(g * 8, (g + 1) * 8) for g in range(WIDTH // 8)]
    loads = []
    for g, rows in enumerate(groups):
        loads.append(
            [
                pltpu.make_async_copy(u_hbm.at[:, :, rows], u.at[:, :, rows], ins.at[0, g]),
                pltpu.make_async_copy(r_hbm.at[:, :, rows], r.at[:, :, rows], ins.at[1, g]),
            ]
        )
        for load in loads[-1]:
            load.start()
    count = jnp.where(row < ROWS // 2, 0.0, 1.0)
    spread = []
    for p0 in range(2):
        wh, wl = weights(w_ref, row, 8 + p0, LOST, 0, count)
        spread.append(jnp.concatenate([wh, wh, wl], axis=1))
    group = lax.broadcasted_iota(jnp.int32, (8, HALF), 1) // WIDTH
    sends = []
    for g, rows in enumerate(groups):
        for half in range(2):
            lanes = slice(half * HALF, (half + 1) * HALF)
            x = [back[half * 16 + c, rows, :] for c in range(16)]
            for bit in (1, 2, 4, 8):
                upper = (group // bit) % 2 == 1
                for c in range(16):
                    if not c & bit:
                        low, high = x[c], x[c + bit]
                        x[c] = jnp.where(upper, pltpu.roll(high, bit * WIDTH, 1), low)
                        x[c + bit] = jnp.where(upper, high, pltpu.roll(low, HALF - bit * WIDTH, 1))
            if half == 0:
                for load in loads[g]:
                    load.wait()
            for p0 in range(2):
                sh, sl = halves(jnp.concatenate(x[p0 * LOST : (p0 + 1) * LOST], axis=0))
                stacked = jnp.concatenate([sh, sl, sh], axis=0)
                total = lax.dot_general(spread[p0], stacked, NN, preferred_element_type=F32)
                total = total.reshape(OCC, 8, HALF)
                out[p0, :, rows, lanes] = u[p0, :, rows, lanes] + total * r[p0, :, rows, lanes]
        sends.append(pltpu.make_async_copy(out.at[:, :, rows], o_ref.at[:, :, rows], outs.at[g]))
        sends[-1].start()
    for send in sends:
        send.wait()


def finish(row, back, w, u, r):
    return pl.pallas_call(
        finish_kernel,
        out_shape=jax.ShapeDtypeStruct(u.shape, F32),
        in_specs=[SMEM, VMEM, VMEM, HBM, HBM],
        out_specs=HBM,
        scratch_shapes=[pltpu.VMEM(u.shape, F32)] * 3
        + [pltpu.SemaphoreType.DMA((2, WIDTH // 8)), pltpu.SemaphoreType.DMA((WIDTH // 8,))],
        compiler_params=pltpu.CompilerParams(vmem_limit_bytes=54_000_000),
        name="finish",
    )(row, back, w, u, r)


def on_device(amplitudes, first_rotation, second_rotation, pair_weights, denominators):
    row = lax.axis_index("occi")
    column = lax.axis_index("occj")
    p = 2 * row + column // OCC
    ahead = jnp.mod(column % OCC - p, OCC)
    wins = ((ahead >= 1) & (ahead <= 7)) | ((ahead == 8) & (p < 8))
    mode = jnp.where(ahead == 0, 2, jnp.where(wins, 0, 1)).astype(jnp.int32).reshape(1)
    row_here = row.astype(jnp.int32).reshape(1)

    z = transform(mode, amplitudes[0], first_rotation, second_rotation)
    z = lax.all_to_all(z.reshape(COLS, WIDTH, VIRT), "occj", split_axis=0, concat_axis=0, tiled=True)
    z = z.reshape(2, ROWS, 2, WIDTH, VIRT)
    e = lax.all_to_all(jnp.swapaxes(z, 0, 1), "occi", split_axis=0, concat_axis=0, tiled=True)
    lost = lost_items(row_here, z, e)
    back = lax.all_to_all(lost.reshape(COLS, WIDTH, HALF), "occj", split_axis=0, concat_axis=0, tiled=True)
    u, r = kept_items(row_here, z, e, pair_weights, denominators)
    return finish(row_here, back, pair_weights, u, r)


def solution(mesh):
    placed = (P(("occi", "occj"), None, None), P(), P(), P(), P("occi", None, "occj", None))
    return jax.shard_map(
        on_device,
        mesh=mesh,
        in_specs=placed,
        out_specs=P("occi", None, "occj", None),
        check_vma=False,
    )
```

```python
import jax
import jax.numpy as jnp
from jax import lax
from jax.experimental import pallas as pl
from jax.experimental.pallas import tpu as pltpu
from jax.sharding import PartitionSpec as P

OCC = 16
VIRT = 768
ROWS = 8
COLS = 32
WIDTH = VIRT // COLS
HALF = VIRT // 2
CHUNK = 256
PARTS = VIRT // CHUNK
KEPT = 9
LOST = 8
F32 = jnp.float32
BF16 = jnp.bfloat16
NT = (((1,), (1,)), ((), ()))
NN = (((1,), (0,)), ((), ()))
HBM = pl.BlockSpec(memory_space=pltpu.HBM)
VMEM = pl.BlockSpec(memory_space=pltpu.VMEM)
SMEM = pl.BlockSpec(memory_space=pltpu.SMEM)


def halves(x):
    high = x.astype(BF16)
    return high, (x - high.astype(F32)).astype(BF16)


def dot3(lh, ll, rh, rl, dims):
    def one(a, b):
        return lax.dot_general(a, b, dims, preferred_element_type=F32)

    return one(lh, rh) + (one(lh, rl) + one(ll, rh))


def transform_kernel(mode_ref, t_ref, a_ref, b_ref, z, t, a, b, t3, a3, pair, ins):
    mode = mode_ref[0]
    mine = jnp.where(mode == 0, 1, 0)
    chunks = [slice(i * CHUNK, (i + 1) * CHUNK) for i in range(PARTS)]
    thirds = [slice(i * VIRT, (i + 1) * VIRT) for i in range(3)]
    loads = []
    for n, (src, dst) in enumerate(((t_ref, t), (a_ref, a), (b_ref, b))):
        loads.append([pltpu.make_async_copy(src.at[r], dst.at[r], ins.at[n, i]) for i, r in enumerate(chunks)])
    for load in loads[0] + loads[1]:
        load.start()

    def put(slot, rows, x, right):
        h, l = halves(x)
        pair[slot, rows, thirds[0]] = h
        pair[slot, rows, thirds[1]] = jnp.where(right, l, h)
        pair[slot, rows, thirds[2]] = jnp.where(right, h, l)

    for i, (load, r) in enumerate(zip(loads[0], chunks)):
        load.wait()
        h, l = halves(t[r, :])
        for n, x in enumerate((h, l, h)):
            t3[n * VIRT + i * CHUNK : n * VIRT + (i + 1) * CHUNK, :] = x
    for load in loads[2]:
        load.start()
    for i, r in enumerate(chunks):
        loads[1][i].wait()
        early = range(2 * (i - 1), min(2 * i, PARTS)) if i else ()
        for j in early:
            loads[2][j].wait()
        h, l = halves(a[r, :])
        for third, x in zip(thirds, (h, h, l)):
            a3[r, third] = x
        for j in early:
            put(1 - mine, chunks[j], b[chunks[j], :], mode != 0)
        put(mine, r, lax.dot_general(a3[r, :], t3[...], NN, preferred_element_type=F32), mode == 0)
    for r in chunks:
        z[r, :] = lax.dot_general(pair[0, r, :], pair[1], NT, preferred_element_type=F32)

    @pl.when(mode == 2)
    def _():
        tiles = [slice(i * 128, (i + 1) * 128) for i in range(VIRT // 128)]
        for n, i in enumerate(tiles):
            for j in tiles[n:]:
                mean = 0.5 * (z[i, j] + z[j, i].T)
                z[i, j] = mean
                if i != j:
                    z[j, i] = mean.T


def transform(mode, t, a, b):
    return pl.pallas_call(
        transform_kernel,
        out_shape=jax.ShapeDtypeStruct((VIRT, VIRT), F32),
        in_specs=[SMEM, HBM, HBM, HBM],
        out_specs=VMEM,
        scratch_shapes=[pltpu.VMEM((VIRT, VIRT), F32)] * 3
        + [pltpu.VMEM((3 * VIRT, VIRT), BF16), pltpu.VMEM((VIRT, 3 * VIRT), BF16), pltpu.VMEM((2, VIRT, 3 * VIRT), BF16)]
        + [pltpu.SemaphoreType.DMA((3, PARTS))],
        compiler_params=pltpu.CompilerParams(vmem_limit_bytes=54_000_000),
        name="transform",
    )(mode, t, a, b)


def sums_kernel(row_ref, z_ref, e_ref, o_ref, s_ref, stage):
    row = row_ref[0]
    for p0 in range(2):
        for m in range(LOST):
            partner = 8 + p0 + m
            there, q0 = lax.rem(row + (partner // 2) % ROWS, ROWS), partner % 2
            at = (p0 * LOST + m) * WIDTH
            stage[at : at + WIDTH, :] = z_ref[p0, there, q0] + e_ref[there, q0, p0]
    for i in range(PARTS):
        rows = slice(i * CHUNK, (i + 1) * CHUNK)
        o_ref[rows, :] = stage[:, rows].T
    for p0 in range(2):
        for m in range(KEPT):
            there, q0 = lax.rem(row + (p0 + m) // 2, ROWS), (p0 + m) % 2
            s_ref[p0, m] = z_ref[p0, there, q0] + e_ref[there, q0, p0]


def row_sums(row, z, e):
    return pl.pallas_call(
        sums_kernel,
        out_shape=(
            jax.ShapeDtypeStruct((VIRT, HALF), F32),
            jax.ShapeDtypeStruct((2, KEPT, WIDTH, VIRT), F32),
        ),
        in_specs=[SMEM, VMEM, VMEM],
        out_specs=(VMEM, VMEM),
        scratch_shapes=[pltpu.VMEM((HALF, VIRT), F32)],
        compiler_params=pltpu.CompilerParams(vmem_limit_bytes=48_000_000),
        name="row_sums",
    )(row, z, e)


def weights(w_ref, row, first, many, tie, count):
    def iota(shape, dim):
        return lax.broadcasted_iota(jnp.int32, shape, dim)

    out = OCC * 8
    pick = (iota((out, OCC), 0) // 8 == iota((out, OCC), 1)).astype(F32)
    m = iota((OCC, many * 8), 1) // 8
    index = (m + (first + 2 * row)) % OCC
    chosen = jnp.where(iota((OCC, many * 8), 0) == index, jnp.where(m == tie, count, 1.0), 0.0)
    full = lax.dot_general(pick, w_ref[...], NT, precision=lax.Precision.HIGHEST, preferred_element_type=F32)
    full = lax.dot_general(full, chosen, NN, precision=lax.Precision.HIGHEST, preferred_element_type=F32)
    same = iota((out, many * 8), 0) % 8 == iota((out, many * 8), 1) % 8
    return halves(jnp.where(same, full, 0.0))


def kept_kernel(row_ref, s_ref, w_ref, d_ref, u_ref, r_ref):
    row = row_ref[0]
    count = jnp.where(row < ROWS // 2, 1.0, 0.0)
    for p0 in range(2):
        wh, wl = weights(w_ref, row, p0, KEPT, KEPT - 1, count)
        for g in range(WIDTH // 8):
            rows = slice(g * 8, (g + 1) * 8)
            sh, sl = halves(s_ref[p0, :, rows, :].reshape(KEPT * 8, VIRT))
            total = dot3(wh, wl, sh, sl, NN).reshape(OCC, 8, VIRT)
            scale = 1.0 / d_ref[p0, :, rows, :]
            r_ref[p0, :, rows, :] = scale
            u_ref[p0, :, rows, :] = total * scale


def kept_items(row, kept, w, d):
    shape = jax.ShapeDtypeStruct(d.shape, F32)
    return pl.pallas_call(
        kept_kernel,
        out_shape=(shape, shape),
        in_specs=[SMEM] + [VMEM] * 3,
        out_specs=(VMEM, VMEM),
        compiler_params=pltpu.CompilerParams(vmem_limit_bytes=40 * 2**20),
        cost_estimate=pl.CostEstimate(flops=2 * 10**9, bytes_accessed=12 * 10**6, transcendentals=0),
        name="kept_items",
    )(row, kept, w, d)


def finish_kernel(row_ref, back, w_ref, u_hbm, r_hbm, o_ref, u, r, out, ins, outs):
    row = row_ref[0]
    groups = [slice(g * 8, (g + 1) * 8) for g in range(WIDTH // 8)]
    loads = []
    for g, rows in enumerate(groups):
        loads.append(
            [
                pltpu.make_async_copy(u_hbm.at[:, :, rows], u.at[:, :, rows], ins.at[0, g]),
                pltpu.make_async_copy(r_hbm.at[:, :, rows], r.at[:, :, rows], ins.at[1, g]),
            ]
        )
        for load in loads[-1]:
            load.start()
    count = jnp.where(row < ROWS // 2, 0.0, 1.0)
    spread = []
    for p0 in range(2):
        wh, wl = weights(w_ref, row, 8 + p0, LOST, 0, count)
        spread.append(jnp.concatenate([wh, wh, wl], axis=1))
    group = lax.broadcasted_iota(jnp.int32, (8, HALF), 1) // WIDTH
    sends = []
    for g, rows in enumerate(groups):
        for half in range(2):
            lanes = slice(half * HALF, (half + 1) * HALF)
            x = [back[half * 16 + c, rows, :] for c in range(16)]
            for bit in (1, 2, 4, 8):
                upper = (group // bit) % 2 == 1
                for c in range(16):
                    if not c & bit:
                        low, high = x[c], x[c + bit]
                        x[c] = jnp.where(upper, pltpu.roll(high, bit * WIDTH, 1), low)
                        x[c + bit] = jnp.where(upper, high, pltpu.roll(low, HALF - bit * WIDTH, 1))
            if half == 0:
                for load in loads[g]:
                    load.wait()
            for p0 in range(2):
                sh, sl = halves(jnp.concatenate(x[p0 * LOST : (p0 + 1) * LOST], axis=0))
                stacked = jnp.concatenate([sh, sl, sh], axis=0)
                total = lax.dot_general(spread[p0], stacked, NN, preferred_element_type=F32)
                total = total.reshape(OCC, 8, HALF)
                out[p0, :, rows, lanes] = u[p0, :, rows, lanes] + total * r[p0, :, rows, lanes]
        sends.append(pltpu.make_async_copy(out.at[:, :, rows], o_ref.at[:, :, rows], outs.at[g]))
        sends[-1].start()
    for send in sends:
        send.wait()


def finish(row, back, w, u, r):
    return pl.pallas_call(
        finish_kernel,
        out_shape=jax.ShapeDtypeStruct(u.shape, F32),
        in_specs=[SMEM, VMEM, VMEM, HBM, HBM],
        out_specs=HBM,
        scratch_shapes=[pltpu.VMEM(u.shape, F32)] * 3
        + [pltpu.SemaphoreType.DMA((2, WIDTH // 8)), pltpu.SemaphoreType.DMA((WIDTH // 8,))],
        compiler_params=pltpu.CompilerParams(vmem_limit_bytes=54_000_000),
        name="finish",
    )(row, back, w, u, r)


def on_device(amplitudes, first_rotation, second_rotation, pair_weights, denominators):
    row = lax.axis_index("occi")
    column = lax.axis_index("occj")
    p = 2 * row + column // OCC
    ahead = jnp.mod(column % OCC - p, OCC)
    wins = ((ahead >= 1) & (ahead <= 7)) | ((ahead == 8) & (p < 8))
    mode = jnp.where(ahead == 0, 2, jnp.where(wins, 0, 1)).astype(jnp.int32).reshape(1)
    row_here = row.astype(jnp.int32).reshape(1)

    z = transform(mode, amplitudes[0], first_rotation, second_rotation)
    z = lax.all_to_all(z.reshape(COLS, WIDTH, VIRT), "occj", split_axis=0, concat_axis=0, tiled=True)
    z = z.reshape(2, ROWS, 2, WIDTH, VIRT)
    e = lax.all_to_all(jnp.swapaxes(z, 0, 1), "occi", split_axis=0, concat_axis=0, tiled=True)
    lost, kept = row_sums(row_here, z, e)
    back = lax.all_to_all(lost.reshape(COLS, WIDTH, HALF), "occj", split_axis=0, concat_axis=0, tiled=True)
    u, r = kept_items(row_here, kept, pair_weights, denominators)
    return finish(row_here, back, pair_weights, u, r)


def solution(mesh):
    placed = (P(("occi", "occj"), None, None), P(), P(), P(), P("occi", None, "occj", None))
    return jax.shard_map(
        on_device,
        mesh=mesh,
        in_specs=placed,
        out_specs=P("occi", None, "occj", None),
        check_vma=False,
    )
```

```python
import jax
import jax.numpy as jnp
from jax import lax
from jax.experimental import pallas as pl
from jax.experimental.pallas import tpu as pltpu
from jax.sharding import PartitionSpec as P

OCC = 16
VIRT = 768
ROWS = 8
COLS = 32
WIDTH = VIRT // COLS
HALF = VIRT // 2
CHUNK = 256
PARTS = VIRT // CHUNK
KEPT = 9
LOST = 8
F32 = jnp.float32
BF16 = jnp.bfloat16
NT = (((1,), (1,)), ((), ()))
NN = (((1,), (0,)), ((), ()))
HBM = pl.BlockSpec(memory_space=pltpu.HBM)
VMEM = pl.BlockSpec(memory_space=pltpu.VMEM)
SMEM = pl.BlockSpec(memory_space=pltpu.SMEM)


def halves(x):
    high = x.astype(BF16)
    return high, (x - high.astype(F32)).astype(BF16)


def dot3(lh, ll, rh, rl, dims):
    def one(a, b):
        return lax.dot_general(a, b, dims, preferred_element_type=F32)

    return one(lh, rh) + (one(lh, rl) + one(ll, rh))


def transform_kernel(mode_ref, t_ref, a_ref, b_ref, z, t, a, b, t3, a3, pair, ins):
    mode = mode_ref[0]
    mine = jnp.where(mode == 0, 1, 0)
    chunks = [slice(i * CHUNK, (i + 1) * CHUNK) for i in range(PARTS)]
    thirds = [slice(i * VIRT, (i + 1) * VIRT) for i in range(3)]
    loads = []
    for n, (src, dst) in enumerate(((t_ref, t), (a_ref, a), (b_ref, b))):
        loads.append([pltpu.make_async_copy(src.at[r], dst.at[r], ins.at[n, i]) for i, r in enumerate(chunks)])
    for load in loads[0] + loads[1]:
        load.start()

    def put(slot, rows, x, right):
        h, l = halves(x)
        pair[slot, rows, thirds[0]] = h
        pair[slot, rows, thirds[1]] = jnp.where(right, l, h)
        pair[slot, rows, thirds[2]] = jnp.where(right, h, l)

    for i, (load, r) in enumerate(zip(loads[0], chunks)):
        load.wait()
        h, l = halves(t[r, :])
        for n, x in enumerate((h, l, h)):
            t3[n * VIRT + i * CHUNK : n * VIRT + (i + 1) * CHUNK, :] = x
    for load in loads[2]:
        load.start()
    for i, r in enumerate(chunks):
        loads[1][i].wait()
        early = range(2 * (i - 1), min(2 * i, PARTS)) if i else ()
        for j in early:
            loads[2][j].wait()
        h, l = halves(a[r, :])
        for third, x in zip(thirds, (h, h, l)):
            a3[r, third] = x
        for j in early:
            put(1 - mine, chunks[j], b[chunks[j], :], mode != 0)
        put(mine, r, lax.dot_general(a3[r, :], t3[...], NN, preferred_element_type=F32), mode == 0)
    for r in chunks:
        z[r, :] = lax.dot_general(pair[0, r, :], pair[1], NT, preferred_element_type=F32)

    @pl.when(mode == 2)
    def _():
        tiles = [slice(i * 128, (i + 1) * 128) for i in range(VIRT // 128)]
        for n, i in enumerate(tiles):
            for j in tiles[n:]:
                mean = 0.5 * (z[i, j] + z[j, i].T)
                z[i, j] = mean
                if i != j:
                    z[j, i] = mean.T


def transform(mode, t, a, b):
    return pl.pallas_call(
        transform_kernel,
        out_shape=jax.ShapeDtypeStruct((VIRT, VIRT), F32),
        in_specs=[SMEM, HBM, HBM, HBM],
        out_specs=VMEM,
        scratch_shapes=[pltpu.VMEM((VIRT, VIRT), F32)] * 3
        + [pltpu.VMEM((3 * VIRT, VIRT), BF16), pltpu.VMEM((VIRT, 3 * VIRT), BF16), pltpu.VMEM((2, VIRT, 3 * VIRT), BF16)]
        + [pltpu.SemaphoreType.DMA((3, PARTS))],
        compiler_params=pltpu.CompilerParams(vmem_limit_bytes=54_000_000),
        name="transform",
    )(mode, t, a, b)


def sums_kernel(row_ref, z_ref, e_ref, o_hbm, s, stage, o, outs):
    row = row_ref[0]
    sends = []
    for p0 in range(2):
        for m in range(LOST):
            partner = 8 + p0 + m
            there, q0 = lax.rem(row + (partner // 2) % ROWS, ROWS), partner % 2
            at = (p0 * LOST + m) * WIDTH
            stage[at : at + WIDTH, :] = z_ref[p0, there, q0] + e_ref[there, q0, p0]
    for i in range(PARTS):
        rows = slice(i * CHUNK, (i + 1) * CHUNK)
        o[rows, :] = stage[:, rows].T
        sends.append(pltpu.make_async_copy(o.at[rows], o_hbm.at[rows], outs.at[i]))
        sends[-1].start()
    for p0 in range(2):
        for m in range(KEPT):
            there, q0 = lax.rem(row + (p0 + m) // 2, ROWS), (p0 + m) % 2
            s[p0, m] = z_ref[p0, there, q0] + e_ref[there, q0, p0]
    for copy in sends:
        copy.wait()


def row_sums(row, z, e):
    return pl.pallas_call(
        sums_kernel,
        out_shape=(
            jax.ShapeDtypeStruct((VIRT, HALF), F32),
            jax.ShapeDtypeStruct((2, KEPT, WIDTH, VIRT), F32),
        ),
        in_specs=[SMEM, VMEM, VMEM],
        out_specs=(HBM, VMEM),
        scratch_shapes=[
            pltpu.VMEM((HALF, VIRT), F32),
            pltpu.VMEM((VIRT, HALF), F32),
            pltpu.SemaphoreType.DMA((PARTS,)),
        ],
        compiler_params=pltpu.CompilerParams(vmem_limit_bytes=48_000_000),
        name="row_sums",
    )(row, z, e)


def weights(w_ref, row, first, many, tie, count):
    def iota(shape, dim):
        return lax.broadcasted_iota(jnp.int32, shape, dim)

    out = OCC * 8
    pick = (iota((out, OCC), 0) // 8 == iota((out, OCC), 1)).astype(F32)
    m = iota((OCC, many * 8), 1) // 8
    index = (m + (first + 2 * row)) % OCC
    chosen = jnp.where(iota((OCC, many * 8), 0) == index, jnp.where(m == tie, count, 1.0), 0.0)
    full = lax.dot_general(pick, w_ref[...], NT, precision=lax.Precision.HIGHEST, preferred_element_type=F32)
    full = lax.dot_general(full, chosen, NN, precision=lax.Precision.HIGHEST, preferred_element_type=F32)
    same = iota((out, many * 8), 0) % 8 == iota((out, many * 8), 1) % 8
    return halves(jnp.where(same, full, 0.0))


def kept_kernel(row_ref, s_ref, w_ref, d_ref, u_ref, r_ref):
    row = row_ref[0]
    count = jnp.where(row < ROWS // 2, 1.0, 0.0)
    for p0 in range(2):
        wh, wl = weights(w_ref, row, p0, KEPT, KEPT - 1, count)
        for g in range(WIDTH // 8):
            rows = slice(g * 8, (g + 1) * 8)
            sh, sl = halves(s_ref[p0, :, rows, :].reshape(KEPT * 8, VIRT))
            total = dot3(wh, wl, sh, sl, NN).reshape(OCC, 8, VIRT)
            scale = 1.0 / d_ref[p0, :, rows, :]
            r_ref[p0, :, rows, :] = scale
            u_ref[p0, :, rows, :] = total * scale


def kept_items(row, kept, w, d):
    shape = jax.ShapeDtypeStruct(d.shape, F32)
    return pl.pallas_call(
        kept_kernel,
        out_shape=(shape, shape),
        in_specs=[SMEM] + [VMEM] * 3,
        out_specs=(VMEM, VMEM),
        compiler_params=pltpu.CompilerParams(vmem_limit_bytes=40 * 2**20),
        cost_estimate=pl.CostEstimate(flops=2 * 10**9, bytes_accessed=12 * 10**6, transcendentals=0),
        name="kept_items",
    )(row, kept, w, d)


def finish_kernel(row_ref, back, w_ref, u_hbm, r_hbm, o_ref, u, r, out, ins, outs):
    row = row_ref[0]
    groups = [slice(g * 8, (g + 1) * 8) for g in range(WIDTH // 8)]
    loads = []
    for g, rows in enumerate(groups):
        loads.append(
            [
                pltpu.make_async_copy(u_hbm.at[:, :, rows], u.at[:, :, rows], ins.at[0, g]),
                pltpu.make_async_copy(r_hbm.at[:, :, rows], r.at[:, :, rows], ins.at[1, g]),
            ]
        )
        for load in loads[-1]:
            load.start()
    count = jnp.where(row < ROWS // 2, 0.0, 1.0)
    spread = []
    for p0 in range(2):
        wh, wl = weights(w_ref, row, 8 + p0, LOST, 0, count)
        spread.append(jnp.concatenate([wh, wh, wl], axis=1))
    group = lax.broadcasted_iota(jnp.int32, (8, HALF), 1) // WIDTH
    sends = []
    for g, rows in enumerate(groups):
        for half in range(2):
            lanes = slice(half * HALF, (half + 1) * HALF)
            x = [back[half * 16 + c, rows, :] for c in range(16)]
            for bit in (1, 2, 4, 8):
                upper = (group // bit) % 2 == 1
                for c in range(16):
                    if not c & bit:
                        low, high = x[c], x[c + bit]
                        x[c] = jnp.where(upper, pltpu.roll(high, bit * WIDTH, 1), low)
                        x[c + bit] = jnp.where(upper, high, pltpu.roll(low, HALF - bit * WIDTH, 1))
            if half == 0:
                for load in loads[g]:
                    load.wait()
            for p0 in range(2):
                sh, sl = halves(jnp.concatenate(x[p0 * LOST : (p0 + 1) * LOST], axis=0))
                stacked = jnp.concatenate([sh, sl, sh], axis=0)
                total = lax.dot_general(spread[p0], stacked, NN, preferred_element_type=F32)
                total = total.reshape(OCC, 8, HALF)
                out[p0, :, rows, lanes] = u[p0, :, rows, lanes] + total * r[p0, :, rows, lanes]
        sends.append(pltpu.make_async_copy(out.at[:, :, rows], o_ref.at[:, :, rows], outs.at[g]))
        sends[-1].start()
    for send in sends:
        send.wait()


def finish(row, back, w, u, r):
    return pl.pallas_call(
        finish_kernel,
        out_shape=jax.ShapeDtypeStruct(u.shape, F32),
        in_specs=[SMEM, VMEM, VMEM, HBM, HBM],
        out_specs=HBM,
        scratch_shapes=[pltpu.VMEM(u.shape, F32)] * 3
        + [pltpu.SemaphoreType.DMA((2, WIDTH // 8)), pltpu.SemaphoreType.DMA((WIDTH // 8,))],
        compiler_params=pltpu.CompilerParams(vmem_limit_bytes=54_000_000),
        name="finish",
    )(row, back, w, u, r)


def on_device(amplitudes, first_rotation, second_rotation, pair_weights, denominators):
    row = lax.axis_index("occi")
    column = lax.axis_index("occj")
    p = 2 * row + column // OCC
    ahead = jnp.mod(column % OCC - p, OCC)
    wins = ((ahead >= 1) & (ahead <= 7)) | ((ahead == 8) & (p < 8))
    mode = jnp.where(ahead == 0, 2, jnp.where(wins, 0, 1)).astype(jnp.int32).reshape(1)
    row_here = row.astype(jnp.int32).reshape(1)

    z = transform(mode, amplitudes[0], first_rotation, second_rotation)
    z = lax.all_to_all(z.reshape(COLS, WIDTH, VIRT), "occj", split_axis=0, concat_axis=0, tiled=True)
    z = z.reshape(2, ROWS, 2, WIDTH, VIRT)
    e = lax.all_to_all(jnp.swapaxes(z, 0, 1), "occi", split_axis=0, concat_axis=0, tiled=True)
    lost, kept = row_sums(row_here, z, e)
    back = lax.all_to_all(lost.reshape(COLS, WIDTH, HALF), "occj", split_axis=0, concat_axis=0, tiled=True)
    u, r = kept_items(row_here, kept, pair_weights, denominators)
    return finish(row_here, back, pair_weights, u, r)


def solution(mesh):
    placed = (P(("occi", "occj"), None, None), P(), P(), P(), P("occi", None, "occj", None))
    return jax.shard_map(
        on_device,
        mesh=mesh,
        in_specs=placed,
        out_specs=P("occi", None, "occj", None),
        check_vma=False,
    )
```
